32 devices in a mesh: groups: 2 (over x), replica: 8 (over z, y), tensor: 2 (over core).
Axes of the slice: x: 2, y: 2, z: 4, core: 2. Of those that a mesh axis runs over, the one named last changes fastest.
Arguments:
- features: bfloat16 [768, 8192], P(('groups', 'replica'), 'tensor'), parts along dimension 0, may hold values from -6 to 6
- value_matrix: bfloat16 [8192, 512], P('tensor'), may hold values from -0.0625 to 0.0625
- adapter_down: bfloat16 [32, 16, 8192], P('replica', None, 'tensor'), may hold values from -0.0625 to 0.0625
- adapter_up: bfloat16 [32, 16, 512], P('replica', None, 'tensor'), may hold values from -0.75 to 0.75
- queries: bfloat16 [768, 4096], P(('groups', 'replica'), 'tensor'), parts along dimension 0, may hold values from -200 to 200
- new_key_rows: bfloat16 [768, 512], P(('groups', 'replica'), 'tensor'), parts along dimension 0, may hold values from -6 to 6
- stored_key_cache: bfloat16 [768, 128, 512], P(('groups', 'replica'), None, 'tensor'), parts along dimension 0, may hold values from -6 to 6
- stored_value_cache: bfloat16 [768, 128, 512], P(('groups', 'replica'), None, 'tensor'), parts along dimension 0, may hold values from -6 to 6
- cache_length: int32 [768], P(('groups', 'replica')), parts along dimension 0, may hold values from 2 to 128, as said below
- resident_adapter_index: int32 [384], P(('groups', 'replica')), parts along dimension 0, may hold values from 0 to 3
- panel_owner_slot: int32 [384], P(('groups', 'replica')), parts along dimension 0, may hold values from 0 to 15, as said below
- outgoing_rows: int32 [16, 8, 2], P(('groups', 'replica')), parts along dimension 0, may hold values from 0 to 3, as said below
- outgoing_counts: int32 [16, 8], P(('groups', 'replica')), parts along dimension 0, may hold values from 0 to 2, as said below
Outputs:
- new_value_rows: bfloat16 [768, 512], P(('groups', 'replica'), 'tensor'), parts along dimension 0
- attended: bfloat16 [768, 4096], P(('groups', 'replica'), 'tensor'), parts along dimension 0
The draws below stay inside these ranges and needn't reach their ends.
There are 2 independent parts, one for each index of `groups`. The reference program is written for one: setup_inputs(seed, part) draws one part's arguments, and reference() takes and returns one part's arrays. A program takes and returns all parts, laid end to end along the dimension named above; an argument that names none is the same for every part. Nothing has to cross between parts.
Inputs may be any that keep to these rules, and one draw needn't show every extreme that they name: `cache_length`: each replica holds a request with 128 cached positions. For every new request, its slot panel_owner_slot % 2 is below the send count of the list of owner panel_owner_slot // 2 for the request's replica. The new requests of one replica take panels from exactly 8 distinct owners, 3 requests from each. The first outgoing_counts[o, h] entries of outgoing_rows[o, h] are distinct; later entries are arbitrary indices in range. `outgoing_counts`: every replica has a list with 2 live entries from some owner.
All inputs are finite; a program needn't handle non-finite values.
Results may differ from the reference program's by a relative error of at most 0.0051.
Values may be sent and summed in bfloat16 or wider, within the bound.
A program may use at most 128 MiB of HBM per device.

```python
import jax
import jax.numpy as jnp
from jax import lax

MODEL_WIDTH = 8192
HD = 128
ADAPTER_RANK = 16
PANEL_SLOTS = 2
REQ_DEV = 48
CTX = 128
ADP_DEV = 4
REPLICAS = 8
REQUEST_TOTAL = 384
HALF = 24
RSLOTS = 3
NEW = 192
ADAPTER_TOTAL = 32
KEY_VALUE_COLS = 512
QW = 4096


def shared_keys(key):
    return jnp.clip(jax.random.normal(key, (REQUEST_TOTAL, CTX, KEY_VALUE_COLS), jnp.float32), -6.0, 6.0)


def draw_stored_key_cache(key, part):
    base_keys = shared_keys(key)
    return base_keys.astype(jnp.bfloat16)


def draw_queries(key, part):
    key = jax.random.fold_in(key, 12)
    drawn = jnp.clip(jax.random.normal(key, (REQUEST_TOTAL, QW), jnp.float32), -6.0, 6.0)
    return drawn.astype(jnp.bfloat16)


def draw_cache_length(key, part):
    key = jax.random.fold_in(key, 31)
    highs = jax.random.randint(jax.random.fold_in(key, 1), (REPLICAS, 1), CTX // 4, CTX + 1)
    lengths = jax.random.randint(jax.random.fold_in(key, 2), (REPLICAS, REQ_DEV), 2, highs + 1)
    top_pick = jax.random.randint(jax.random.fold_in(key, 3), (REPLICAS,), 0, REQ_DEV)
    lengths = lengths.at[jnp.arange(REPLICAS), top_pick].set(CTX)
    return lengths.reshape(REQUEST_TOTAL).astype(jnp.int32)


def routing_plan(key):
    group_count = HALF // RSLOTS
    holder_keys = jax.random.split(jax.random.fold_in(key, 41), REPLICAS)

    def perm_for(subkey):
        return jax.random.permutation(subkey, REPLICAS)
    perms = jax.vmap(perm_for)(holder_keys)
    last_owner = REPLICAS - 1
    where_last = jnp.argmax(perms[0] == last_owner)
    first_row = perms[0].at[where_last].set(perms[0, 0]).at[0].set(last_owner)
    perms = perms.at[0].set(first_row)
    owners = perms[:, :group_count]
    pair_keys = jax.random.split(jax.random.fold_in(key, 42), REPLICAS * group_count)

    def pair_for(subkey):
        return jax.random.permutation(subkey, ADP_DEV)[:2]
    pairs = jax.vmap(pair_for)(pair_keys).reshape(REPLICAS, group_count, 2)
    picks = jax.random.randint(jax.random.fold_in(key, 43), (REPLICAS, group_count, RSLOTS), 0, 2)
    picks = picks.at[:, :, 0].set(0)
    picks = picks.at[:, :, 1].set(1)
    live_counts = 1 + jnp.max(picks, axis=2)
    slots_drawn = (owners[:, :, None] * PANEL_SLOTS + picks).reshape(REPLICAS, HALF)
    order_keys = jax.random.split(jax.random.fold_in(key, 44), REPLICAS)

    def order_for(subkey):
        return jax.random.permutation(subkey, HALF)
    orders = jax.vmap(order_for)(order_keys)
    slots_drawn = jnp.take_along_axis(slots_drawn, orders, axis=1)
    holder_grid = jnp.broadcast_to(jnp.arange(REPLICAS)[:, None], owners.shape)
    padding = jax.random.randint(jax.random.fold_in(key, 45), (REPLICAS, REPLICAS, PANEL_SLOTS), 0, ADP_DEV)
    lists = padding.at[owners, holder_grid].set(pairs)
    counts = jnp.zeros((REPLICAS, REPLICAS), jnp.int32).at[owners, holder_grid].set(live_counts)
    return (slots_drawn.reshape(NEW).astype(jnp.int32), lists.astype(jnp.int32), counts.astype(jnp.int32))


def draw_panel_owner_slot(key, part):
    return routing_plan(key)[0]


def draw_outgoing_rows(key, part):
    return routing_plan(key)[1]


def draw_outgoing_counts(key, part):
    return routing_plan(key)[2]


def plant(values, rng, least, top_value):
    shape = values.shape
    place = [jax.random.randint(jax.random.fold_in(rng, axis), (), 0, shape[axis]) for axis in range(len(shape))]
    values = values.at[tuple(place)].set(least)
    longest = shape.index(max(shape))
    place[longest] = (place[longest] + 1) % shape[longest]
    return values.at[tuple(place)].set(top_value)


def steps_of(own_key, dims, cuts, smallest, top_value):
    gain, own = 1.0, jax.random.fold_in(own_key, 6)
    for position, blocks in cuts:
        steps = jnp.exp(jax.random.uniform(jax.random.fold_in(own, position), (blocks,), jnp.float32, smallest / len(cuts), top_value / len(cuts)))
        gain = gain * jnp.repeat(steps, dims[position] // blocks).reshape([-1 if axis == position else 1 for axis in range(len(dims))])
    return gain


def gaussian(key, extent, spread, reach, cuts=(), kind=jnp.bfloat16):
    values = spread * jax.random.normal(key, extent, jnp.float32)
    if cuts:
        values = values * steps_of(key, extent, cuts, -0.22, 0.18)
    return jnp.clip(values, -reach, reach).astype(kind)


def setup_inputs(seed: int = 0, part: int = 0) -> dict:
    seeds = jax.random.split(jax.random.key(seed), 14)
    part_splits = jax.random.split(jax.random.fold_in(seeds[13], part), 14)
    return {
        "features": gaussian(part_splits[0], (REQUEST_TOTAL, MODEL_WIDTH), 1.0, 6.0, ((0, 8), (1, 2))),
        "value_matrix": gaussian(seeds[1], (MODEL_WIDTH, KEY_VALUE_COLS), MODEL_WIDTH ** -0.5, 0.0625, ((0, 2),)),
        "adapter_down": gaussian(seeds[2], (ADAPTER_TOTAL, ADAPTER_RANK, MODEL_WIDTH), MODEL_WIDTH ** -0.5, 0.0625, ((0, 8), (2, 2))),
        "adapter_up": gaussian(seeds[3], (ADAPTER_TOTAL, ADAPTER_RANK, KEY_VALUE_COLS), (ADAPTER_RANK * 4) ** -0.5, 0.75, ((0, 8), (2, 2))),
        "queries": draw_queries(jax.random.fold_in(jax.random.fold_in(seeds[13], part), 71), part),
        "new_key_rows": gaussian(part_splits[5], (REQUEST_TOTAL, KEY_VALUE_COLS), 1.0, 6.0, ((0, 8), (1, 2))),
        "stored_key_cache": draw_stored_key_cache(jax.random.fold_in(jax.random.fold_in(seeds[13], part), 71), part),
        "stored_value_cache": gaussian(part_splits[7], (REQUEST_TOTAL, CTX, KEY_VALUE_COLS), 1.0, 6.0, ((0, 8), (2, 2))),
        "cache_length": draw_cache_length(jax.random.fold_in(jax.random.fold_in(seeds[13], part), 71), part),
        "resident_adapter_index": plant(jax.random.randint(part_splits[9], (NEW,), 0, ADP_DEV), jax.random.fold_in(part_splits[9], 1), 0, ADP_DEV - 1).astype(jnp.int32),
        "panel_owner_slot": draw_panel_owner_slot(jax.random.fold_in(jax.random.fold_in(seeds[13], part), 71), part),
        "outgoing_rows": draw_outgoing_rows(jax.random.fold_in(jax.random.fold_in(seeds[13], part), 71), part),
        "outgoing_counts": draw_outgoing_counts(jax.random.fold_in(jax.random.fold_in(seeds[13], part), 71), part),
    }


ADAPTER_SCALE = 2.0

def attend(queries, new_key_rows, stored_key_cache, stored_value_cache, new_value_rows, cache_length):
    row_count = queries.shape[0]
    kv_count = new_key_rows.shape[1] // HD
    group_size = queries.shape[1] // new_key_rows.shape[1]
    query_heads = queries.astype(jnp.float32).reshape(row_count, kv_count, group_size, HD)
    cached_keys = stored_key_cache.astype(jnp.float32).reshape(row_count, CTX, kv_count, HD)
    cached_values = stored_value_cache.astype(jnp.float32).reshape(row_count, CTX, kv_count, HD)
    fresh_keys = new_key_rows.astype(jnp.float32).reshape(row_count, kv_count, HD)
    fresh_values = new_value_rows.astype(jnp.float32).reshape(row_count, kv_count, HD)
    scale = 1.0 / jnp.sqrt(jnp.float32(HD))
    scores = jnp.einsum('rghd,rpgd->rghp', query_heads, cached_keys) * scale
    fresh_scores = jnp.einsum('rghd,rgd->rgh', query_heads, fresh_keys) * scale
    valid_mask = (jnp.arange(CTX, dtype=jnp.int32)[None, :] < cache_length[:, None])[:, None, None, :]
    masked = jnp.where(valid_mask, scores, -jnp.inf)
    top_score = jnp.maximum(lax.optimization_barrier(jnp.max(masked, axis=3)), fresh_scores)
    raw_weights = jnp.where(valid_mask, jnp.exp(scores - top_score[..., None]), 0.0)
    fresh_raw = jnp.exp(fresh_scores - top_score)
    norm_total = lax.optimization_barrier(jnp.sum(raw_weights, axis=3)) + fresh_raw
    weights = (raw_weights / norm_total[..., None]).astype(jnp.bfloat16)
    fresh_weights = (fresh_raw / norm_total).astype(jnp.bfloat16)
    result_sum = jnp.einsum('rghp,rpgd->rghd', weights.astype(jnp.float32), cached_values)
    result_sum = result_sum + fresh_weights.astype(jnp.float32)[..., None] * fresh_values[:, :, None, :]
    return result_sum.astype(jnp.bfloat16).reshape(row_count, queries.shape[1])

def reference(features, value_matrix, adapter_down, adapter_up, queries, new_key_rows, stored_key_cache, stored_value_cache, cache_length, resident_adapter_index, panel_owner_slot, outgoing_rows, outgoing_counts):
    base_portion = jnp.dot(features, value_matrix, preferred_element_type=jnp.float32)
    holders = jnp.arange(REPLICAS, dtype=jnp.int32)[:, None]
    resident_ids = resident_adapter_index.reshape(REPLICAS, HALF) + holders * ADP_DEV
    slot_pairs = panel_owner_slot.reshape(REPLICAS, HALF)
    owners = slot_pairs // PANEL_SLOTS
    slot_index = slot_pairs % PANEL_SLOTS
    holder_grid = jnp.broadcast_to(holders, owners.shape)
    local_ids = outgoing_rows[owners, holder_grid, slot_index]
    live_mask = slot_index < outgoing_counts[owners, holder_grid]
    incoming_ids = owners * ADP_DEV + local_ids
    adapter_index = jnp.concatenate([resident_ids, incoming_ids], axis=1).astype(jnp.int32)
    keep_mask = jnp.concatenate([jnp.ones_like(live_mask), live_mask], axis=1)
    feature_blocks = features.reshape(REPLICAS, REQ_DEV, MODEL_WIDTH)

    def shrink_block(pieces):
        block_rows, block_index = pieces
        down_matrices = jnp.take(adapter_down, block_index, axis=0).astype(jnp.float32)
        return jnp.einsum('rd,rkd->rk', block_rows.astype(jnp.float32), down_matrices, precision=lax.Precision.HIGHEST)
    shrunk_input = lax.map(shrink_block, (feature_blocks, adapter_index)).reshape(REQUEST_TOTAL, ADAPTER_RANK)
    shrunk_input = jnp.where(keep_mask.reshape(REQUEST_TOTAL, 1), shrunk_input, jnp.zeros((), jnp.float32))
    up_matrices = jnp.take(adapter_up, adapter_index.reshape(REQUEST_TOTAL), axis=0).astype(jnp.float32)
    adapter_output = jnp.einsum('sj,sjo->so', shrunk_input, up_matrices, precision=lax.Precision.HIGHEST)
    new_value_rows = (base_portion + ADAPTER_SCALE * adapter_output).astype(jnp.bfloat16)

    def attend_block(pieces):
        return attend(*pieces)
    attended = lax.map(attend_block, (queries.reshape(REPLICAS, REQ_DEV, QW), new_key_rows.reshape(REPLICAS, REQ_DEV, KEY_VALUE_COLS), stored_key_cache.reshape(REPLICAS, REQ_DEV, CTX, KEY_VALUE_COLS), stored_value_cache.reshape(REPLICAS, REQ_DEV, CTX, KEY_VALUE_COLS), new_value_rows.reshape(REPLICAS, REQ_DEV, KEY_VALUE_COLS), cache_length.reshape(REPLICAS, REQ_DEV))).reshape(REQUEST_TOTAL, QW)
    return (new_value_rows, attended)
```

```python
import functools
import math

import jax
import jax.numpy as jnp
from jax import lax
from jax.experimental import pallas as pl
from jax.experimental.pallas import tpu as pltpu
from jax.sharding import PartitionSpec as P

HD = 128
PANEL_SLOTS = 2
ADAPTER_SCALE = 2.0
MESH = pl.DeviceIdType.MESH
F32, BF16, I32 = jnp.float32, jnp.bfloat16, jnp.int32
NT = (((1,), (1,)), ((), ()))
RANKS = 4
CHUNKS = 4


def iota(shape, axis):
    return lax.broadcasted_iota(I32, shape, axis)


def dot(a, b, dims=(((1,), (0,)), ((), ()))):
    return lax.dot_general(a, b, dims, preferred_element_type=F32)


def split(x):
    high = x.astype(BF16)
    return high, (x - high.astype(F32)).astype(BF16)


def spread(ref, count, shape, axis, first):
    index = iota(shape, axis)
    out = jnp.full(shape, -1, I32)
    for i in range(count):
        out = jnp.where(index == first + i, ref[i], out)
    return out


def kernel(
    replicas, per_pair, pieces,
    feat_hbm, vm_hbm, down_hbm, up_hbm, q_hbm, nk_hbm, k_hbm, v_hbm,
    len_ref, res_ref, slot_ref, rows_ref, count_ref,
    nv_ref, att_ref,
    feat, vm, down, up, q, nk, kc, vc,
    x32, tx, rx, half_tx, half_rx, shr_tx, shr_rx, ret_tx, ret_rx,
    q3, nk3, sc, wt, fresh, acc,
    in_sem, vm_sem, k_sem, v_sem, tx_sem, rx_sem, ret_tx_sem, ret_rx_sem, peer_sem,
):
    me = lax.axis_index("replica")
    core = lax.axis_index("tensor")
    rows, width = feat.shape
    half = res_ref.shape[0]
    adapters, rank, _ = down.shape
    flat = adapters * rank
    cols = up.shape[2]
    kv = nk.shape[1] // HD
    heads = q.shape[1] // HD
    group = heads // kv
    ctx = kc.shape[1]
    piece = width // pieces
    sent = replicas * per_pair
    block = PANEL_SLOTS * RANKS
    step = rows // CHUNKS
    depth = width // CHUNKS

    def load(src, dst, sem):
        copy = pltpu.make_async_copy(src, dst, sem)
        copy.start()
        return copy

    feat_in = load(feat_hbm, feat, in_sem.at[0])
    down_in = load(down_hbm, down, in_sem.at[1])
    vm_in = [
        load(vm_hbm.at[pl.ds(c * depth, depth)], vm.at[pl.ds(c * depth, depth)], vm_sem.at[c])
        for c in range(CHUNKS)
    ]
    q_in = load(q_hbm, q, in_sem.at[2])
    nk_in = load(nk_hbm, nk, in_sem.at[3])
    k_in = [
        load(k_hbm.at[pl.ds(c * step, step)], kc.at[pl.ds(c * step, step)], k_sem.at[c])
        for c in range(CHUNKS)
    ]
    up_in = load(up_hbm, up, in_sem.at[4])
    v_in = [
        load(v_hbm.at[pl.ds(c * step, step)], vc.at[pl.ds(c * step, step)], v_sem.at[c])
        for c in range(CHUNKS)
    ]

    barrier = pltpu.get_barrier_semaphore()
    for d in range(1, replicas):
        pl.semaphore_signal(
            barrier, inc=1, device_id={"replica": lax.rem(me + d, replicas)}, device_id_type=MESH
        )
    pl.semaphore_signal(barrier, inc=1, device_id={"tensor": 1 - core}, device_id_type=MESH)

    square = (rows, rows)
    sub, lane = iota(square, 0), iota(square, 1)
    slot_l = spread(slot_ref, half, square, 1, half)
    slot_s = spread(slot_ref, half, square, 0, half)
    own_l, own_s = slot_l >> 1, slot_s >> 1
    same = own_l == own_s
    number_l = jnp.sum(jnp.where(same & (sub < lane), 1.0, 0.0), axis=0, keepdims=True).astype(I32)
    number_s = jnp.sum(jnp.where(same & (lane < sub), 1.0, 0.0), axis=1, keepdims=True).astype(I32)
    goes = jnp.where(lane[:1] >= half, own_l[:1] * per_pair + number_l, -1)
    chooser = jnp.where(iota((sent, rows), 0) == goes, 1.0, 0.0).astype(BF16)
    comes = own_s[:, :1] * block + (slot_s[:, :1] & 1) * RANKS + number_s
    comes = jnp.where(sub[:, :1] >= half, comes, -1)
    picker = jnp.where(iota((rows, replicas * block), 1) == comes, 1.0, 0.0).astype(BF16)

    feat_in.wait()
    chosen = dot(chooser, feat[...])
    lanes = piece // HD
    for p in range(pieces):
        for b in range(lanes):
            at = p * piece + b * HD
            x32[b, pl.ds(p, sent, stride=pieces), :] = chosen[:, at : at + HD]
    for b in range(lanes):
        tx[:, :, b * HD : (b + 1) * HD] = x32[b].astype(BF16).reshape(replicas, -1, HD)

    pl.semaphore_wait(barrier, replicas)
    out_copies = []
    for d in range(1, replicas):
        there = lax.rem(me + d, replicas)
        copy = pltpu.make_async_remote_copy(
            src_ref=tx.at[there], dst_ref=rx.at[me],
            send_sem=tx_sem.at[d], recv_sem=rx_sem.at[d],
            device_id={"replica": there}, device_id_type=MESH,
        )
        copy.start()
        out_copies.append(copy)
    rx[me] = tx[me]

    down_in.wait()
    shrunk = dot(feat[...], down[...].reshape(flat, width), NT)
    res_s = spread(res_ref, half, (rows, flat), 0, 0)
    shrunk = jnp.where((iota((rows, flat), 1) // rank) == res_s, shrunk, 0.0)[:half]
    base = jnp.zeros((rows, 2 * cols), F32)
    for c in range(CHUNKS):
        vm_in[c].wait()
        base += dot(feat[:, c * depth : (c + 1) * depth], vm[c * depth : (c + 1) * depth, :])
    padded = jnp.concatenate([shrunk, jnp.zeros((half, cols - flat), F32)], axis=1)
    for t in range(2):
        half_tx[t, :rows] = base[:, t * cols : (t + 1) * cols]
        half_tx[t, rows:] = padded
    half_copy = pltpu.make_async_remote_copy(
        src_ref=half_tx.at[1 - core], dst_ref=half_rx,
        send_sem=peer_sem.at[0], recv_sem=peer_sem.at[1],
        device_id={"tensor": 1 - core}, device_id_type=MESH,
    )
    half_copy.start()

    q_in.wait()
    nk_in.wait()
    for h in range(heads):
        g = h // group
        q3[pl.ds(h, rows, stride=heads), :] = q[:, h * HD : (h + 1) * HD].astype(F32)
        nk3[pl.ds(h, rows, stride=heads), :] = nk[:, g * HD : (g + 1) * HD].astype(F32)
    scale = 1.0 / math.sqrt(HD)
    head_of = iota((heads, HD), 0) // group
    place = iota((heads, ctx), 1)
    unroll = 6

    def score(base_row):
        for u in range(unroll):
            r = base_row + u
            rows_r = q3[pl.ds(pl.multiple_of(r * heads, heads), heads), :]
            wide = jnp.concatenate(
                [jnp.where(head_of == g, rows_r, 0.0) for g in range(kv)], axis=1
            ).astype(BF16)
            s = dot(wide, kc[r], NT) * scale
            sc[r] = jnp.where(place < len_ref[r], s, -jnp.inf)

    for c in range(CHUNKS):
        k_in[c].wait()
        lax.fori_loop(
            0, step // unroll, lambda i, _, c=c: score(c * step + i * unroll), None
        )

    for copy in out_copies:
        copy.wait_recv()
    for b in range(lanes):
        x32[b] = rx[:, :, b * HD : (b + 1) * HD].reshape(sent * pieces, HD).astype(F32)
    foreign = jnp.zeros((sent, flat), F32)
    for p in range(pieces):
        x_p = [x32[b, pl.ds(p, sent, stride=pieces), :] for b in range(lanes)]
        x_p = jnp.concatenate(x_p, axis=1).astype(BF16)
        foreign += dot(x_p, down[:, :, p * piece : (p + 1) * piece].reshape(flat, piece), NT)
    shr_tx[...] = jnp.concatenate([foreign, jnp.zeros((sent, HD - flat), F32)], axis=1)
    shr_copy = pltpu.make_async_remote_copy(
        src_ref=shr_tx, dst_ref=shr_rx,
        send_sem=peer_sem.at[2], recv_sem=peer_sem.at[3],
        device_id={"tensor": 1 - core}, device_id_type=MESH,
    )
    shr_copy.start()

    def soften(c):
        r = pl.ds(c * step, step)
        flat_r = pl.ds(c * step * heads, step * heads)
        s = sc[r].reshape(step * heads, ctx)
        fs = jnp.sum(q3[flat_r, :] * nk3[flat_r, :], axis=1, keepdims=True) * scale
        top = jnp.maximum(jnp.max(s, axis=1, keepdims=True), fs)
        w = jnp.exp(s - top)
        fw = jnp.exp(fs - top)
        inverse = 1.0 / (jnp.sum(w, axis=1, keepdims=True) + fw)
        wt[r] = (w * inverse).astype(BF16).reshape(step, heads, ctx)
        fw = (fw * inverse).astype(BF16).astype(F32)
        fresh[flat_r, :] = jnp.broadcast_to(fw, (step * heads, HD))

    for c in range(CHUNKS):
        soften(c)

    up_in.wait()
    shape = (replicas * block, flat)
    sub, lane = iota(shape, 0), iota(shape, 1)
    adapter = jnp.full(shape, -1, I32)
    for i in range(replicas):
        for s in range(PANEL_SLOTS):
            at = (sub // RANKS) == i * PANEL_SLOTS + s
            value = jnp.where(s < count_ref[0, i], rows_ref[0, i, s], -1)
            adapter = jnp.where(at, value, adapter)
    shape = (replicas * block, sent)
    sub_e, lane_e = iota(shape, 0), iota(shape, 1)
    place_e = sub_e & (RANKS - 1)
    expand = ((sub_e // block) * per_pair + place_e == lane_e) & (place_e < per_pair)
    expand = jnp.where(expand, 1.0, 0.0).astype(BF16)
    up_flat = up[...].reshape(flat, cols)
    shr_copy.wait_recv()
    high, low = split(shr_tx[:, :flat] + shr_rx[:, :flat])
    keep = (lane // rank) == adapter
    high = jnp.where(keep, dot(expand, high), 0.0).astype(BF16)
    low = jnp.where(keep, dot(expand, low), 0.0).astype(BF16)
    ret_tx[...] = (dot(high, up_flat) + dot(low, up_flat)).reshape(ret_tx.shape)
    ret_copies = []
    for d in range(1, replicas):
        there = lax.rem(me + d, replicas)
        copy = pltpu.make_async_remote_copy(
            src_ref=ret_tx.at[there], dst_ref=ret_rx.at[me],
            send_sem=ret_tx_sem.at[d], recv_sem=ret_rx_sem.at[d],
            device_id={"replica": there}, device_id_type=MESH,
        )
        copy.start()
        ret_copies.append(copy)
    ret_rx[me] = ret_tx[me]

    def gather(base_row):
        for u in range(unroll):
            r = base_row + u
            mixed = dot(wt[r], vc[r])
            out = mixed[:, :HD]
            for g in range(1, kv):
                out = jnp.where(head_of == g, mixed[:, g * HD : (g + 1) * HD], out)
            acc[pl.ds(pl.multiple_of(r * heads, heads), heads), :] = out

    for c in range(CHUNKS):
        v_in[c].wait()
        lax.fori_loop(
            0, step // unroll, lambda i, _, c=c: gather(c * step + i * unroll), None
        )

    half_copy.wait_recv()
    both = half_tx[core] + half_rx[...]
    high, low = split(both[rows:, :flat])
    resident = dot(high, up_flat) + dot(low, up_flat)
    resident = jnp.concatenate([resident, jnp.zeros((rows - half, cols), F32)], axis=0)
    for copy in ret_copies:
        copy.wait_recv()
    high, low = split(ret_rx[...].reshape(replicas * block, cols))
    adapted = resident + (dot(picker, high) + dot(picker, low))
    values = (both[:rows] + ADAPTER_SCALE * adapted).astype(BF16)
    nv_ref[...] = values
    values = values.astype(F32)
    for h in range(heads):
        g = h // group
        at = pl.ds(h, rows, stride=heads)
        out = acc[at, :] + fresh[at, :] * values[:, g * HD : (g + 1) * HD]
        att_ref[:, h * HD : (h + 1) * HD] = out.astype(BF16)

    for copy in out_copies + ret_copies + [half_copy, shr_copy]:
        copy.wait_send()


def body(
    features, value_matrix, adapter_down, adapter_up, queries, new_key_rows, stored_key_cache,
    stored_value_cache, cache_length, resident_adapter_index, panel_owner_slot, outgoing_rows,
    outgoing_counts,
):
    replicas = lax.axis_size("replica")
    rows, width = features.shape
    half = resident_adapter_index.shape[0]
    cols = adapter_up.shape[2]
    heads = queries.shape[1] // HD
    ctx = stored_key_cache.shape[1]
    per_pair = max(2, -(-half // replicas))
    pieces = 16 // math.gcd(16, per_pair)
    sent = replicas * per_pair
    block = PANEL_SLOTS * RANKS
    anywhere = pl.BlockSpec(memory_space=pl.ANY)
    scalars = pl.BlockSpec(memory_space=pltpu.SMEM)
    vmem = pl.BlockSpec(memory_space=pltpu.VMEM)
    big = [features, value_matrix, adapter_down, adapter_up, queries, new_key_rows,
           stored_key_cache, stored_value_cache]
    dma = pltpu.SemaphoreType.DMA
    chunk = (replicas, per_pair * pieces, width // pieces)
    return pl.pallas_call(
        functools.partial(kernel, replicas, per_pair, pieces),
        out_shape=(
            jax.ShapeDtypeStruct((rows, cols), BF16),
            jax.ShapeDtypeStruct(queries.shape, BF16),
        ),
        in_specs=[anywhere] * 8 + [scalars] * 5,
        out_specs=(vmem, vmem),
        scratch_shapes=[pltpu.VMEM(a.shape, BF16) for a in big] + [
            pltpu.VMEM((width // pieces // HD, sent * pieces, HD), F32),
            pltpu.VMEM(chunk, BF16),
            pltpu.VMEM(chunk, BF16),
            pltpu.VMEM((2, rows + half, cols), F32),
            pltpu.VMEM((rows + half, cols), F32),
            pltpu.VMEM((sent, HD), F32),
            pltpu.VMEM((sent, HD), F32),
            pltpu.VMEM((replicas, block, cols), F32),
            pltpu.VMEM((replicas, block, cols), F32),
            pltpu.VMEM((rows * heads, HD), F32),
            pltpu.VMEM((rows * heads, HD), F32),
            pltpu.VMEM((rows, heads, ctx), F32),
            pltpu.VMEM((rows, heads, ctx), BF16),
            pltpu.VMEM((rows * heads, HD), F32),
            pltpu.VMEM((rows * heads, HD), F32),
            dma((5,)), dma((CHUNKS,)), dma((CHUNKS,)), dma((CHUNKS,)),
            dma((replicas,)), dma((replicas,)), dma((replicas,)), dma((replicas,)), dma((4,)),
        ],
        compiler_params=pltpu.CompilerParams(
            collective_id=0, has_side_effects=True, vmem_limit_bytes=48 * 1024 * 1024
        ),
        cost_estimate=pl.CostEstimate(
            flops=500_000_000, bytes_accessed=12_000_000, transcendentals=100_000
        ),
    )(*big, cache_length, resident_adapter_index, panel_owner_slot, outgoing_rows, outgoing_counts)


def solution(mesh):
    in_specs = (
        P(("groups", "replica"), "tensor"),
        P("tensor", None),
        P("replica", None, "tensor"),
        P("replica", None, "tensor"),
        P(("groups", "replica"), "tensor"),
        P(("groups", "replica"), "tensor"),
        P(("groups", "replica"), None, "tensor"),
        P(("groups", "replica"), None, "tensor"),
        P(("groups", "replica")),
        P(("groups", "replica")),
        P(("groups", "replica")),
        P(("groups", "replica"), None, None),
        P(("groups", "replica"), None),
    )
    out_specs = (P(("groups", "replica"), "tensor"), P(("groups", "replica"), "tensor"))
    return jax.shard_map(body, mesh=mesh, in_specs=in_specs, out_specs=out_specs, check_vma=False)
```

```python
import functools
import math

import jax
import jax.numpy as jnp
from jax import lax
from jax.experimental import pallas as pl
from jax.experimental.pallas import tpu as pltpu
from jax.sharding import PartitionSpec as P

HD = 128
PANEL_SLOTS = 2
ADAPTER_SCALE = 2.0
MESH = pl.DeviceIdType.MESH
F32, BF16, I32 = jnp.float32, jnp.bfloat16, jnp.int32
NT = (((1,), (1,)), ((), ()))
RANKS = 4
CHUNKS = 4


def iota(shape, axis):
    return lax.broadcasted_iota(I32, shape, axis)


def dot(a, b, dims=(((1,), (0,)), ((), ()))):
    return lax.dot_general(a, b, dims, preferred_element_type=F32)


def split(x):
    high = x.astype(BF16)
    return high, (x - high.astype(F32)).astype(BF16)


def spread(ref, count, shape, axis, first):
    index = iota(shape, axis)
    out = jnp.full(shape, -1, I32)
    for i in range(count):
        out = jnp.where(index == first + i, ref[i], out)
    return out


def kernel(
    replicas, per_pair, pieces,
    feat_hbm, vm_hbm, down_hbm, up_hbm, q_hbm, nk_hbm, k_hbm, v_hbm,
    len_ref, res_ref, slot_ref, rows_ref, count_ref,
    nv_ref, att_ref,
    feat, vm, down, up, q, nk, kc, vc,
    x32, tx, rx, half_tx, half_rx, shr_tx, shr_rx, ret_tx, ret_rx,
    q3, nk3, sc, wt, fresh, acc,
    in_sem, vm_sem, k_sem, v_sem, tx_sem, rx_sem, ret_tx_sem, ret_rx_sem, peer_sem,
):
    me = lax.axis_index("replica")
    core = lax.axis_index("tensor")
    rows, width = feat.shape
    half = res_ref.shape[0]
    adapters, rank, _ = down.shape
    flat = adapters * rank
    cols = up.shape[2]
    kv = nk.shape[1] // HD
    heads = q.shape[1] // HD
    group = heads // kv
    ctx = kc.shape[1]
    piece = width // pieces
    sent = replicas * per_pair
    block = PANEL_SLOTS * RANKS
    step = rows // CHUNKS
    depth = width // CHUNKS

    def load(src, dst, sem):
        copy = pltpu.make_async_copy(src, dst, sem)
        copy.start()
        return copy

    feat_in = load(feat_hbm, feat, in_sem.at[0])
    down_in = load(down_hbm, down, in_sem.at[1])
    vm_in = [
        load(vm_hbm.at[pl.ds(c * depth, depth)], vm.at[pl.ds(c * depth, depth)], vm_sem.at[c])
        for c in range(CHUNKS)
    ]
    q_in = load(q_hbm, q, in_sem.at[2])
    nk_in = load(nk_hbm, nk, in_sem.at[3])
    k_in = [
        load(k_hbm.at[pl.ds(c * step, step)], kc.at[pl.ds(c * step, step)], k_sem.at[c])
        for c in range(CHUNKS)
    ]
    up_in = load(up_hbm, up, in_sem.at[4])
    v_in = [
        load(v_hbm.at[pl.ds(c * step, step)], vc.at[pl.ds(c * step, step)], v_sem.at[c])
        for c in range(CHUNKS)
    ]

    barrier = pltpu.get_barrier_semaphore()
    for d in range(1, replicas):
        pl.semaphore_signal(
            barrier, inc=1, device_id={"replica": lax.rem(me + d, replicas)}, device_id_type=MESH
        )
    pl.semaphore_signal(barrier, inc=1, device_id={"tensor": 1 - core}, device_id_type=MESH)

    square = (rows, rows)
    sub, lane = iota(square, 0), iota(square, 1)
    slot_l = spread(slot_ref, half, square, 1, half)
    slot_s = spread(slot_ref, half, square, 0, half)
    own_l, own_s = slot_l >> 1, slot_s >> 1
    same = own_l == own_s
    number_l = jnp.sum(jnp.where(same & (sub < lane), 1.0, 0.0), axis=0, keepdims=True).astype(I32)
    number_s = jnp.sum(jnp.where(same & (lane < sub), 1.0, 0.0), axis=1, keepdims=True).astype(I32)
    goes = jnp.where(lane[:1] >= half, own_l[:1] * per_pair + number_l, -1)
    chooser = jnp.where(iota((sent, rows), 0) == goes, 1.0, 0.0).astype(BF16)
    comes = own_s[:, :1] * block + (slot_s[:, :1] & 1) * RANKS + number_s
    comes = jnp.where(sub[:, :1] >= half, comes, -1)
    picker = jnp.where(iota((rows, replicas * block), 1) == comes, 1.0, 0.0).astype(BF16)

    feat_in.wait()
    chosen = dot(chooser, feat[...])
    lanes = piece // HD
    for p in range(pieces):
        for b in range(lanes):
            at = p * piece + b * HD
            x32[b, pl.ds(p, sent, stride=pieces), :] = chosen[:, at : at + HD]
    for b in range(lanes):
        tx[:, :, b * HD : (b + 1) * HD] = x32[b].astype(BF16).reshape(replicas, -1, HD)

    pl.semaphore_wait(barrier, replicas)
    out_copies = []
    for d in range(1, replicas):
        there = lax.rem(me + d, replicas)
        copy = pltpu.make_async_remote_copy(
            src_ref=tx.at[there], dst_ref=rx.at[me],
            send_sem=tx_sem.at[d], recv_sem=rx_sem.at[d],
            device_id={"replica": there}, device_id_type=MESH,
        )
        copy.start()
        out_copies.append(copy)
    rx[me] = tx[me]

    down_in.wait()
    shrunk = dot(feat[...], down[...].reshape(flat, width), NT)
    res_s = spread(res_ref, half, (rows, flat), 0, 0)
    shrunk = jnp.where((iota((rows, flat), 1) // rank) == res_s, shrunk, 0.0)[:half]
    base = jnp.zeros((rows, 2 * cols), F32)
    for c in range(CHUNKS):
        vm_in[c].wait()
        base += dot(feat[:, c * depth : (c + 1) * depth], vm[c * depth : (c + 1) * depth, :])
    padded = jnp.concatenate([shrunk, jnp.zeros((half, cols - flat), F32)], axis=1)
    for t in range(2):
        half_tx[t, :rows] = base[:, t * cols : (t + 1) * cols]
        half_tx[t, rows:] = padded
    half_copy = pltpu.make_async_remote_copy(
        src_ref=half_tx.at[1 - core], dst_ref=half_rx,
        send_sem=peer_sem.at[0], recv_sem=peer_sem.at[1],
        device_id={"tensor": 1 - core}, device_id_type=MESH,
    )
    half_copy.start()

    q_in.wait()
    nk_in.wait()
    for h in range(heads):
        g = h // group
        q3[pl.ds(h, rows, stride=heads), :] = q[:, h * HD : (h + 1) * HD].astype(F32)
        nk3[pl.ds(h, rows, stride=heads), :] = nk[:, g * HD : (g + 1) * HD].astype(F32)
    scale = 1.0 / math.sqrt(HD)
    head_of = iota((heads, HD), 0) // group
    place = iota((heads, ctx), 1)
    unroll = 6

    def score(base_row):
        for u in range(unroll):
            r = base_row + u
            rows_r = q3[pl.ds(pl.multiple_of(r * heads, heads), heads), :]
            wide = jnp.concatenate(
                [jnp.where(head_of == g, rows_r, 0.0) for g in range(kv)], axis=1
            ).astype(BF16)
            s = dot(wide, kc[r], NT) * scale
            sc[r] = jnp.where(place < len_ref[r], s, -jnp.inf)

    for c in range(CHUNKS):
        k_in[c].wait()
        lax.fori_loop(
            0, step // unroll, lambda i, _, c=c: score(c * step + i * unroll), None
        )

    for copy in out_copies:
        copy.wait_recv()
    for b in range(lanes):
        x32[b] = rx[:, :, b * HD : (b + 1) * HD].reshape(sent * pieces, HD).astype(F32)
    foreign = jnp.zeros((sent, flat), F32)
    for p in range(pieces):
        x_p = [x32[b, pl.ds(p, sent, stride=pieces), :] for b in range(lanes)]
        x_p = jnp.concatenate(x_p, axis=1).astype(BF16)
        foreign += dot(x_p, down[:, :, p * piece : (p + 1) * piece].reshape(flat, piece), NT)
    shr_tx[...] = jnp.concatenate([foreign, jnp.zeros((sent, HD - flat), F32)], axis=1)
    shr_copy = pltpu.make_async_remote_copy(
        src_ref=shr_tx, dst_ref=shr_rx,
        send_sem=peer_sem.at[2], recv_sem=peer_sem.at[3],
        device_id={"tensor": 1 - core}, device_id_type=MESH,
    )
    shr_copy.start()

    def soften(c):
        r = pl.ds(c * step, step)
        flat_r = pl.ds(c * step * heads, step * heads)
        s = sc[r].reshape(step * heads, ctx)
        fs = jnp.sum(q3[flat_r, :] * nk3[flat_r, :], axis=1, keepdims=True) * scale
        top = jnp.maximum(jnp.max(s, axis=1, keepdims=True), fs)
        w = jnp.exp(s - top)
        fw = jnp.exp(fs - top)
        inverse = 1.0 / (jnp.sum(w, axis=1, keepdims=True) + fw)
        wt[r] = (w * inverse).astype(BF16).reshape(step, heads, ctx)
        fw = (fw * inverse).astype(BF16).astype(F32)
        fresh[flat_r, :] = jnp.broadcast_to(fw, (step * heads, HD))

    for c in range(CHUNKS):
        soften(c)

    up_in.wait()
    shape = (replicas * block, flat)
    sub, lane = iota(shape, 0), iota(shape, 1)
    adapter = jnp.full(shape, -1, I32)
    for i in range(replicas):
        for s in range(PANEL_SLOTS):
            at = (sub // RANKS) == i * PANEL_SLOTS + s
            value = jnp.where(s < count_ref[0, i], rows_ref[0, s, i], -1)
            adapter = jnp.where(at, value, adapter)
    shape = (replicas * block, sent)
    sub_e, lane_e = iota(shape, 0), iota(shape, 1)
    place_e = sub_e & (RANKS - 1)
    expand = ((sub_e // block) * per_pair + place_e == lane_e) & (place_e < per_pair)
    expand = jnp.where(expand, 1.0, 0.0).astype(BF16)
    up_flat = up[...].reshape(flat, cols)
    shr_copy.wait_recv()
    high, low = split(shr_tx[:, :flat] + shr_rx[:, :flat])
    keep = (lane // rank) == adapter
    high = jnp.where(keep, dot(expand, high), 0.0).astype(BF16)
    low = jnp.where(keep, dot(expand, low), 0.0).astype(BF16)
    ret_tx[...] = (dot(high, up_flat) + dot(low, up_flat)).reshape(ret_tx.shape)
    ret_copies = []
    for d in range(1, replicas):
        there = lax.rem(me + d, replicas)
        copy = pltpu.make_async_remote_copy(
            src_ref=ret_tx.at[there], dst_ref=ret_rx.at[me],
            send_sem=ret_tx_sem.at[d], recv_sem=ret_rx_sem.at[d],
            device_id={"replica": there}, device_id_type=MESH,
        )
        copy.start()
        ret_copies.append(copy)
    ret_rx[me] = ret_tx[me]

    def gather(base_row):
        for u in range(unroll):
            r = base_row + u
            mixed = dot(wt[r], vc[r])
            out = mixed[:, :HD]
            for g in range(1, kv):
                out = jnp.where(head_of == g, mixed[:, g * HD : (g + 1) * HD], out)
            acc[pl.ds(pl.multiple_of(r * heads, heads), heads), :] = out

    for c in range(CHUNKS):
        v_in[c].wait()
        lax.fori_loop(
            0, step // unroll, lambda i, _, c=c: gather(c * step + i * unroll), None
        )

    half_copy.wait_recv()
    both = half_tx[core] + half_rx[...]
    high, low = split(both[rows:, :flat])
    resident = dot(high, up_flat) + dot(low, up_flat)
    resident = jnp.concatenate([resident, jnp.zeros((rows - half, cols), F32)], axis=0)
    for copy in ret_copies:
        copy.wait_recv()
    high, low = split(ret_rx[...].reshape(replicas * block, cols))
    adapted = resident + (dot(picker, high) + dot(picker, low))
    values = (both[:rows] + ADAPTER_SCALE * adapted).astype(BF16)
    nv_ref[...] = values
    values = values.astype(F32)
    for h in range(heads):
        g = h // group
        at = pl.ds(h, rows, stride=heads)
        out = acc[at, :] + fresh[at, :] * values[:, g * HD : (g + 1) * HD]
        att_ref[:, h * HD : (h + 1) * HD] = out.astype(BF16)

    for copy in out_copies + ret_copies + [half_copy, shr_copy]:
        copy.wait_send()


def body(
    features, value_matrix, adapter_down, adapter_up, queries, new_key_rows, stored_key_cache,
    stored_value_cache, cache_length, resident_adapter_index, panel_owner_slot, outgoing_rows,
    outgoing_counts,
):
    replicas = lax.axis_size("replica")
    rows, width = features.shape
    half = resident_adapter_index.shape[0]
    cols = adapter_up.shape[2]
    heads = queries.shape[1] // HD
    ctx = stored_key_cache.shape[1]
    per_pair = max(2, -(-half // replicas))
    pieces = 16 // math.gcd(16, per_pair)
    sent = replicas * per_pair
    block = PANEL_SLOTS * RANKS
    anywhere = pl.BlockSpec(memory_space=pl.ANY)
    scalars = pl.BlockSpec(memory_space=pltpu.SMEM)
    vmem = pl.BlockSpec(memory_space=pltpu.VMEM)
    big = [features, value_matrix, adapter_down, adapter_up, queries, new_key_rows,
           stored_key_cache, stored_value_cache]
    dma = pltpu.SemaphoreType.DMA
    chunk = (replicas, per_pair * pieces, width // pieces)
    return pl.pallas_call(
        functools.partial(kernel, replicas, per_pair, pieces),
        out_shape=(
            jax.ShapeDtypeStruct((rows, cols), BF16),
            jax.ShapeDtypeStruct(queries.shape, BF16),
        ),
        in_specs=[anywhere] * 8 + [scalars] * 5,
        out_specs=(vmem, vmem),
        scratch_shapes=[pltpu.VMEM(a.shape, BF16) for a in big] + [
            pltpu.VMEM((width // pieces // HD, sent * pieces, HD), F32),
            pltpu.VMEM(chunk, BF16),
            pltpu.VMEM(chunk, BF16),
            pltpu.VMEM((2, rows + half, cols), F32),
            pltpu.VMEM((rows + half, cols), F32),
            pltpu.VMEM((sent, HD), F32),
            pltpu.VMEM((sent, HD), F32),
            pltpu.VMEM((replicas, block, cols), F32),
            pltpu.VMEM((replicas, block, cols), F32),
            pltpu.VMEM((rows * heads, HD), F32),
            pltpu.VMEM((rows * heads, HD), F32),
            pltpu.VMEM((rows, heads, ctx), F32),
            pltpu.VMEM((rows, heads, ctx), BF16),
            pltpu.VMEM((rows * heads, HD), F32),
            pltpu.VMEM((rows * heads, HD), F32),
            dma((5,)), dma((CHUNKS,)), dma((CHUNKS,)), dma((CHUNKS,)),
            dma((replicas,)), dma((replicas,)), dma((replicas,)), dma((replicas,)), dma((4,)),
        ],
        compiler_params=pltpu.CompilerParams(
            collective_id=0, has_side_effects=True, vmem_limit_bytes=63 * 1024 * 1024
        ),
        cost_estimate=pl.CostEstimate(
            flops=500_000_000, bytes_accessed=12_000_000, transcendentals=100_000
        ),
    )(*big, cache_length, resident_adapter_index, panel_owner_slot,
      jnp.swapaxes(outgoing_rows, 1, 2), outgoing_counts)


def solution(mesh):
    in_specs = (
        P(("groups", "replica"), "tensor"),
        P("tensor", None),
        P("replica", None, "tensor"),
        P("replica", None, "tensor"),
        P(("groups", "replica"), "tensor"),
        P(("groups", "replica"), "tensor"),
        P(("groups", "replica"), None, "tensor"),
        P(("groups", "replica"), None, "tensor"),
        P(("groups", "replica")),
        P(("groups", "replica")),
        P(("groups", "replica")),
        P(("groups", "replica"), None, None),
        P(("groups", "replica"), None),
    )
    out_specs = (P(("groups", "replica"), "tensor"), P(("groups", "replica"), "tensor"))
    return jax.shard_map(body, mesh=mesh, in_specs=in_specs, out_specs=out_specs, check_vma=False)
```

```python
import functools
import math

import jax
import jax.numpy as jnp
from jax import lax
from jax.experimental import pallas as pl
from jax.experimental.pallas import tpu as pltpu
from jax.sharding import PartitionSpec as P

HD = 128
PANEL_SLOTS = 2
ADAPTER_SCALE = 2.0
MESH = pl.DeviceIdType.MESH
F32, BF16, I32 = jnp.float32, jnp.bfloat16, jnp.int32
NT = (((1,), (1,)), ((), ()))
RANKS = 4
CHUNKS = 4


def iota(shape, axis):
    return lax.broadcasted_iota(I32, shape, axis)


def dot(a, b, dims=(((1,), (0,)), ((), ()))):
    return lax.dot_general(a, b, dims, preferred_element_type=F32)


def split(x):
    high = x.astype(BF16)
    return high, (x - high.astype(F32)).astype(BF16)


def spread(ref, count, shape, axis, first):
    index = iota(shape, axis)
    out = jnp.full(shape, -1, I32)
    for i in range(count):
        out = jnp.where(index == first + i, ref[i], out)
    return out


def kernel(
    replicas, per_pair, pieces,
    feat_hbm, vm_hbm, down_hbm, up_hbm, q_hbm, nk_hbm, k_hbm, v_hbm,
    len_hbm, res_hbm, slot_hbm, rows_hbm, count_hbm,
    nv_ref, att_ref,
    feat, vm, down, up, q, nk, kc, vc,
    x32, tx, rx, half_tx, half_rx, shr_tx, shr_rx, ret_tx, ret_rx,
    q3, nk3, sc, wt, fresh, acc,
    len_ref, res_ref, slot_ref, rows_ref, count_ref,
    in_sem, vm_sem, k_sem, v_sem, tx_sem, rx_sem, ret_tx_sem, ret_rx_sem, peer_sem,
):
    me = lax.axis_index("replica")
    core = lax.axis_index("tensor")
    rows, width = feat.shape
    half = res_ref.shape[0]
    adapters, rank, _ = down.shape
    flat = adapters * rank
    cols = up.shape[2]
    kv = nk.shape[1] // HD
    heads = q.shape[1] // HD
    group = heads // kv
    ctx = kc.shape[1]
    piece = width // pieces
    sent = replicas * per_pair
    block = PANEL_SLOTS * RANKS
    step = rows // CHUNKS
    depth = width // CHUNKS

    barrier = pltpu.get_barrier_semaphore()
    for d in range(1, replicas):
        pl.semaphore_signal(
            barrier, inc=1, device_id={"replica": lax.rem(me + d, replicas)}, device_id_type=MESH
        )
    pl.semaphore_signal(barrier, inc=1, device_id={"tensor": 1 - core}, device_id_type=MESH)

    def load(src, dst, sem):
        copy = pltpu.make_async_copy(src, dst, sem)
        copy.start()
        return copy

    slot_in = load(slot_hbm, slot_ref, in_sem.at[5])
    feat_in = load(feat_hbm, feat, in_sem.at[0])
    down_in = load(down_hbm, down, in_sem.at[1])
    vm_in = [
        load(vm_hbm.at[pl.ds(c * depth, depth)], vm.at[pl.ds(c * depth, depth)], vm_sem.at[c])
        for c in range(CHUNKS)
    ]
    q_in = load(q_hbm, q, in_sem.at[2])
    nk_in = load(nk_hbm, nk, in_sem.at[3])
    k_in = [
        load(k_hbm.at[pl.ds(c * step, step)], kc.at[pl.ds(c * step, step)], k_sem.at[c])
        for c in range(CHUNKS)
    ]
    up_in = load(up_hbm, up, in_sem.at[4])
    res_in = load(res_hbm, res_ref, in_sem.at[6])
    len_in = load(len_hbm, len_ref, in_sem.at[7])
    rows_in = load(rows_hbm, rows_ref, in_sem.at[8])
    count_in = load(count_hbm, count_ref, in_sem.at[9])
    v_in = [
        load(v_hbm.at[pl.ds(c * step, step)], vc.at[pl.ds(c * step, step)], v_sem.at[c])
        for c in range(CHUNKS)
    ]

    square = (rows, rows)
    sub, lane = iota(square, 0), iota(square, 1)
    slot_in.wait()
    slot_l = spread(slot_ref, half, (1, rows), 1, half)
    slot_s = jnp.sum(jnp.where(sub == lane, slot_l, 0).astype(F32), axis=1, keepdims=True)
    slot_s = slot_s.astype(I32)
    own_l, own_s = slot_l >> 1, slot_s >> 1
    same = own_l == own_s
    number_l = jnp.sum(jnp.where(same & (sub < lane), 1.0, 0.0), axis=0, keepdims=True).astype(I32)
    number_s = jnp.sum(jnp.where(same & (lane < sub), 1.0, 0.0), axis=1, keepdims=True).astype(I32)
    goes = jnp.where(lane[:1] >= half, own_l * per_pair + number_l, -1)
    chooser = jnp.where(iota((sent, rows), 0) == goes, 1.0, 0.0).astype(BF16)
    comes = own_s * block + (slot_s & 1) * RANKS + number_s
    comes = jnp.where(sub[:, :1] >= half, comes, -1)
    picker = jnp.where(iota((rows, replicas * block), 1) == comes, 1.0, 0.0).astype(BF16)

    feat_in.wait()
    chosen = dot(chooser, feat[...])
    lanes = piece // HD
    for p in range(pieces):
        for b in range(lanes):
            at = p * piece + b * HD
            x32[b, pl.ds(p, sent, stride=pieces), :] = chosen[:, at : at + HD]
    for b in range(lanes):
        tx[:, :, b * HD : (b + 1) * HD] = x32[b].astype(BF16).reshape(replicas, -1, HD)

    pl.semaphore_wait(barrier, replicas)
    out_copies = []
    order = sorted(range(1, replicas), key=lambda d: -abs(2 * d - replicas))
    for d in order:
        there = lax.rem(me + d, replicas)
        copy = pltpu.make_async_remote_copy(
            src_ref=tx.at[there], dst_ref=rx.at[me],
            send_sem=tx_sem.at[d], recv_sem=rx_sem.at[d],
            device_id={"replica": there}, device_id_type=MESH,
        )
        copy.start()
        out_copies.append(copy)
    rx[me] = tx[me]

    down_in.wait()
    shrunk = dot(feat[...], down[...].reshape(flat, width), NT)
    res_in.wait()
    res_s = spread(res_ref, half, (rows, flat), 0, 0)
    shrunk = jnp.where((iota((rows, flat), 1) // rank) == res_s, shrunk, 0.0)[:half]
    base = jnp.zeros((rows, 2 * cols), F32)
    for c in range(CHUNKS):
        vm_in[c].wait()
        base += dot(feat[:, c * depth : (c + 1) * depth], vm[c * depth : (c + 1) * depth, :])
    padded = jnp.concatenate([shrunk, jnp.zeros((half, cols - flat), F32)], axis=1)
    for t in range(2):
        half_tx[t, :rows] = base[:, t * cols : (t + 1) * cols]
        half_tx[t, rows:] = padded
    half_copy = pltpu.make_async_remote_copy(
        src_ref=half_tx.at[1 - core], dst_ref=half_rx,
        send_sem=peer_sem.at[0], recv_sem=peer_sem.at[1],
        device_id={"tensor": 1 - core}, device_id_type=MESH,
    )
    half_copy.start()

    q_in.wait()
    nk_in.wait()
    for h in range(heads):
        g = h // group
        q3[pl.ds(h, rows, stride=heads), :] = q[:, h * HD : (h + 1) * HD].astype(F32)
        nk3[pl.ds(h, rows, stride=heads), :] = nk[:, g * HD : (g + 1) * HD].astype(F32)
    len_in.wait()
    scale = 1.0 / math.sqrt(HD)
    head_of = iota((heads, HD), 0) // group
    place = iota((heads, ctx), 1)
    unroll = 6

    def score(base_row):
        for u in range(unroll):
            r = base_row + u
            rows_r = q3[pl.ds(pl.multiple_of(r * heads, heads), heads), :]
            wide = jnp.concatenate(
                [jnp.where(head_of == g, rows_r, 0.0) for g in range(kv)], axis=1
            ).astype(BF16)
            s = dot(wide, kc[r], NT) * scale
            sc[r] = jnp.where(place < len_ref[r], s, -jnp.inf)

    for c in range(CHUNKS):
        k_in[c].wait()
        lax.fori_loop(
            0, step // unroll, lambda i, _, c=c: score(c * step + i * unroll), None
        )

    for copy in out_copies:
        copy.wait_recv()
    for b in range(lanes):
        x32[b] = rx[:, :, b * HD : (b + 1) * HD].reshape(sent * pieces, HD).astype(F32)
    foreign = jnp.zeros((sent, flat), F32)
    for p in range(pieces):
        x_p = [x32[b, pl.ds(p, sent, stride=pieces), :] for b in range(lanes)]
        x_p = jnp.concatenate(x_p, axis=1).astype(BF16)
        foreign += dot(x_p, down[:, :, p * piece : (p + 1) * piece].reshape(flat, piece), NT)
    shr_tx[...] = jnp.concatenate([foreign, jnp.zeros((sent, HD - flat), F32)], axis=1)
    shr_copy = pltpu.make_async_remote_copy(
        src_ref=shr_tx, dst_ref=shr_rx,
        send_sem=peer_sem.at[2], recv_sem=peer_sem.at[3],
        device_id={"tensor": 1 - core}, device_id_type=MESH,
    )
    shr_copy.start()

    def soften(c):
        r = pl.ds(c * step, step)
        flat_r = pl.ds(c * step * heads, step * heads)
        s = sc[r].reshape(step * heads, ctx)
        fs = jnp.sum(q3[flat_r, :] * nk3[flat_r, :], axis=1, keepdims=True) * scale
        top = jnp.maximum(jnp.max(s, axis=1, keepdims=True), fs)
        w = jnp.exp(s - top)
        fw = jnp.exp(fs - top)
        inverse = 1.0 / (jnp.sum(w, axis=1, keepdims=True) + fw)
        wt[r] = (w * inverse).astype(BF16).reshape(step, heads, ctx)
        fw = (fw * inverse).astype(BF16).astype(F32)
        fresh[flat_r, :] = jnp.broadcast_to(fw, (step * heads, HD))

    for c in range(CHUNKS):
        soften(c)

    up_in.wait()
    rows_in.wait()
    count_in.wait()
    shape = (replicas * block, flat)
    sub, lane = iota(shape, 0), iota(shape, 1)
    adapter = jnp.full(shape, -1, I32)
    for i in range(replicas):
        for s in range(PANEL_SLOTS):
            at = (sub // RANKS) == i * PANEL_SLOTS + s
            value = jnp.where(s < count_ref[0, i], rows_ref[0, s, i], -1)
            adapter = jnp.where(at, value, adapter)
    shape = (replicas * block, sent)
    sub_e, lane_e = iota(shape, 0), iota(shape, 1)
    place_e = sub_e & (RANKS - 1)
    expand = ((sub_e // block) * per_pair + place_e == lane_e) & (place_e < per_pair)
    expand = jnp.where(expand, 1.0, 0.0).astype(BF16)
    up_flat = up[...].reshape(flat, cols)
    shr_copy.wait_recv()
    high, low = split(shr_tx[:, :flat] + shr_rx[:, :flat])
    keep = (lane // rank) == adapter
    high = jnp.where(keep, dot(expand, high), 0.0).astype(BF16)
    low = jnp.where(keep, dot(expand, low), 0.0).astype(BF16)
    ret_tx[...] = (dot(high, up_flat) + dot(low, up_flat)).reshape(ret_tx.shape)
    ret_copies = []
    for d in order:
        there = lax.rem(me + d, replicas)
        copy = pltpu.make_async_remote_copy(
            src_ref=ret_tx.at[there], dst_ref=ret_rx.at[me],
            send_sem=ret_tx_sem.at[d], recv_sem=ret_rx_sem.at[d],
            device_id={"replica": there}, device_id_type=MESH,
        )
        copy.start()
        ret_copies.append(copy)
    ret_rx[me] = ret_tx[me]

    def gather(base_row):
        for u in range(unroll):
            r = base_row + u
            mixed = dot(wt[r], vc[r])
            out = mixed[:, :HD]
            for g in range(1, kv):
                out = jnp.where(head_of == g, mixed[:, g * HD : (g + 1) * HD], out)
            acc[pl.ds(pl.multiple_of(r * heads, heads), heads), :] = out

    for c in range(CHUNKS):
        v_in[c].wait()
        lax.fori_loop(
            0, step // unroll, lambda i, _, c=c: gather(c * step + i * unroll), None
        )

    half_copy.wait_recv()
    both = half_tx[core] + half_rx[...]
    high, low = split(both[rows:, :flat])
    resident = dot(high, up_flat) + dot(low, up_flat)
    resident = jnp.concatenate([resident, jnp.zeros((rows - half, cols), F32)], axis=0)
    for copy in ret_copies:
        copy.wait_recv()
    high, low = split(ret_rx[...].reshape(replicas * block, cols))
    adapted = resident + (dot(picker, high) + dot(picker, low))
    values = (both[:rows] + ADAPTER_SCALE * adapted).astype(BF16)
    nv_ref[...] = values
    values = values.astype(F32)
    for h in range(heads):
        g = h // group
        at = pl.ds(h, rows, stride=heads)
        out = acc[at, :] + fresh[at, :] * values[:, g * HD : (g + 1) * HD]
        att_ref[:, h * HD : (h + 1) * HD] = out.astype(BF16)

    for copy in out_copies + ret_copies + [half_copy, shr_copy]:
        copy.wait_send()


def hand_over(nv_in, att_in, nv_out, att_out):
    nv_out[...] = nv_in[...]
    att_out[...] = att_in[...]


def body(
    features, value_matrix, adapter_down, adapter_up, queries, new_key_rows, stored_key_cache,
    stored_value_cache, cache_length, resident_adapter_index, panel_owner_slot, outgoing_rows,
    outgoing_counts,
):
    replicas = lax.axis_size("replica")
    rows, width = features.shape
    half = resident_adapter_index.shape[0]
    cols = adapter_up.shape[2]
    heads = queries.shape[1] // HD
    ctx = stored_key_cache.shape[1]
    per_pair = max(2, -(-half // replicas))
    pieces = 16 // math.gcd(16, per_pair)
    sent = replicas * per_pair
    block = PANEL_SLOTS * RANKS
    anywhere = pl.BlockSpec(memory_space=pl.ANY)
    vmem = pl.BlockSpec(memory_space=pltpu.VMEM)
    big = [features, value_matrix, adapter_down, adapter_up, queries, new_key_rows,
           stored_key_cache, stored_value_cache]
    small = [cache_length, resident_adapter_index, panel_owner_slot,
             jnp.swapaxes(outgoing_rows, 1, 2), outgoing_counts]
    dma = pltpu.SemaphoreType.DMA
    chunk = (replicas, per_pair * pieces, width // pieces)
    values, attended = pl.pallas_call(
        functools.partial(kernel, replicas, per_pair, pieces),
        out_shape=(
            jax.ShapeDtypeStruct((rows, cols), BF16),
            jax.ShapeDtypeStruct(queries.shape, BF16),
        ),
        in_specs=[anywhere] * 13,
        out_specs=(vmem, vmem),
        scratch_shapes=[pltpu.VMEM(a.shape, BF16) for a in big] + [
            pltpu.VMEM((width // pieces // HD, sent * pieces, HD), F32),
            pltpu.VMEM(chunk, BF16),
            pltpu.VMEM(chunk, BF16),
            pltpu.VMEM((2, rows + half, cols), F32),
            pltpu.VMEM((rows + half, cols), F32),
            pltpu.VMEM((sent, HD), F32),
            pltpu.VMEM((sent, HD), F32),
            pltpu.VMEM((replicas, block, cols), F32),
            pltpu.VMEM((replicas, block, cols), F32),
            pltpu.VMEM((rows * heads, HD), F32),
            pltpu.VMEM((rows * heads, HD), F32),
            pltpu.VMEM((rows, heads, ctx), F32),
            pltpu.VMEM((rows, heads, ctx), BF16),
            pltpu.VMEM((rows * heads, HD), F32),
            pltpu.VMEM((rows * heads, HD), F32),
            *[pltpu.SMEM(a.shape, I32) for a in small],
            dma((10,)), dma((CHUNKS,)), dma((CHUNKS,)), dma((CHUNKS,)),
            dma((replicas,)), dma((replicas,)), dma((replicas,)), dma((replicas,)), dma((4,)),
        ],
        compiler_params=pltpu.CompilerParams(
            collective_id=0, has_side_effects=True, vmem_limit_bytes=63 * 1024 * 1024
        ),
        cost_estimate=pl.CostEstimate(
            flops=500_000_000, bytes_accessed=12_000_000, transcendentals=100_000
        ),
    )(*big, *small)
    return pl.pallas_call(
        hand_over,
        out_shape=(
            jax.ShapeDtypeStruct(values.shape, BF16),
            jax.ShapeDtypeStruct(attended.shape, BF16),
        ),
        in_specs=[vmem] * 2,
        out_specs=(vmem, vmem),

    )(values, attended)


def solution(mesh):
    in_specs = (
        P(("groups", "replica"), "tensor"),
        P("tensor", None),
        P("replica", None, "tensor"),
        P("replica", None, "tensor"),
        P(("groups", "replica"), "tensor"),
        P(("groups", "replica"), "tensor"),
        P(("groups", "replica"), None, "tensor"),
        P(("groups", "replica"), None, "tensor"),
        P(("groups", "replica")),
        P(("groups", "replica")),
        P(("groups", "replica")),
        P(("groups", "replica"), None, None),
        P(("groups", "replica"), None),
    )
    out_specs = (P(("groups", "replica"), "tensor"), P(("groups", "replica"), "tensor"))
    return jax.shard_map(body, mesh=mesh, in_specs=in_specs, out_specs=out_specs, check_vma=False)
```

```python
import functools
import math

import jax
import jax.numpy as jnp
from jax import lax
from jax.experimental import pallas as pl
from jax.experimental.pallas import tpu as pltpu
from jax.sharding import PartitionSpec as P

HD = 128
PANEL_SLOTS = 2
ADAPTER_SCALE = 2.0
MESH = pl.DeviceIdType.MESH
F32, BF16, I32 = jnp.float32, jnp.bfloat16, jnp.int32
NT = (((1,), (1,)), ((), ()))
RANKS = 4
CHUNKS = 4
BATCHES = 2


def iota(shape, axis):
    return lax.broadcasted_iota(I32, shape, axis)


def dot(a, b, dims=(((1,), (0,)), ((), ()))):
    return lax.dot_general(a, b, dims, preferred_element_type=F32)


def split(x):
    high = x.astype(BF16)
    return high, (x - high.astype(F32)).astype(BF16)


def spread(ref, count, shape, axis, first):
    index = iota(shape, axis)
    out = jnp.full(shape, -1, I32)
    for i in range(count):
        out = jnp.where(index == first + i, ref[i], out)
    return out


def kernel(
    replicas, per_pair, pieces,
    feat_hbm, vm_hbm, down_hbm, up_hbm, q_hbm, nk_hbm, k_hbm, v_hbm,
    len_hbm, res_hbm, slot_hbm, rows_hbm, count_hbm,
    nv_ref, att_ref,
    feat, vm, down, up, q, nk, kc, vc,
    x32, tx, rx, half_tx, half_rx, shr_tx, shr_rx, ret_tx, ret_rx,
    q3, nk3, sc, wt, fresh, acc,
    len_ref, res_ref, slot_ref, rows_ref, count_ref,
    in_sem, vm_sem, k_sem, v_sem, tx_sem, rx_sem, ret_tx_sem, ret_rx_sem, peer_sem,
):
    me = lax.axis_index("replica")
    core = lax.axis_index("tensor")
    rows, width = feat.shape
    half = res_ref.shape[0]
    adapters, rank, _ = down.shape
    flat = adapters * rank
    cols = up.shape[2]
    kv = nk.shape[1] // HD
    heads = q.shape[1] // HD
    group = heads // kv
    ctx = kc.shape[1]
    piece = width // pieces
    sent = replicas * per_pair
    block = PANEL_SLOTS * RANKS
    step = rows // CHUNKS
    depth = width // CHUNKS

    barrier = pltpu.get_barrier_semaphore()
    for d in range(1, replicas):
        pl.semaphore_signal(
            barrier, inc=1, device_id={"replica": lax.rem(me + d, replicas)}, device_id_type=MESH
        )
    pl.semaphore_signal(barrier, inc=1, device_id={"tensor": 1 - core}, device_id_type=MESH)

    def load(src, dst, sem):
        copy = pltpu.make_async_copy(src, dst, sem)
        copy.start()
        return copy

    slot_in = load(slot_hbm, slot_ref, in_sem.at[5])
    feat_in = load(feat_hbm, feat, in_sem.at[0])
    down_in = load(down_hbm, down, in_sem.at[1])
    vm_in = [
        load(vm_hbm.at[pl.ds(c * depth, depth)], vm.at[pl.ds(c * depth, depth)], vm_sem.at[c])
        for c in range(CHUNKS)
    ]
    q_in = load(q_hbm, q, in_sem.at[2])
    nk_in = load(nk_hbm, nk, in_sem.at[3])
    k_in = [
        load(k_hbm.at[pl.ds(c * step, step)], kc.at[pl.ds(c * step, step)], k_sem.at[c])
        for c in range(CHUNKS)
    ]
    up_in = load(up_hbm, up, in_sem.at[4])
    res_in = load(res_hbm, res_ref, in_sem.at[6])
    len_in = load(len_hbm, len_ref, in_sem.at[7])
    rows_in = load(rows_hbm, rows_ref, in_sem.at[8])
    count_in = load(count_hbm, count_ref, in_sem.at[9])
    v_in = [
        load(v_hbm.at[pl.ds(c * step, step)], vc.at[pl.ds(c * step, step)], v_sem.at[c])
        for c in range(CHUNKS)
    ]

    order = [0] + sorted(range(1, replicas), key=lambda k: -abs(2 * k - replicas))

    def partner(offset, sign):
        return lax.rem(me + sign * offset + replicas, replicas)

    def slot_of(owner):
        offset = jnp.where(owner < me, owner - me + replicas, owner - me)
        out = jnp.zeros_like(owner)
        for k in range(1, replicas):
            out = jnp.where(offset == order[k], k, out)
        return out

    square = (rows, rows)
    sub, lane = iota(square, 0), iota(square, 1)
    slot_in.wait()
    slot_l = spread(slot_ref, half, (1, rows), 1, half)
    slot_s = jnp.sum(jnp.where(sub == lane, slot_l, 0).astype(F32), axis=1, keepdims=True)
    slot_s = slot_s.astype(I32)
    own_l, own_s = slot_l >> 1, slot_s >> 1
    same = own_l == own_s
    number_l = jnp.sum(jnp.where(same & (sub < lane), 1.0, 0.0), axis=0, keepdims=True).astype(I32)
    number_s = jnp.sum(jnp.where(same & (lane < sub), 1.0, 0.0), axis=1, keepdims=True).astype(I32)
    goes = jnp.where(lane[:1] >= half, slot_of(own_l) * per_pair + number_l, -1)
    chooser = jnp.where(iota((sent, rows), 0) == goes, 1.0, 0.0).astype(BF16)
    comes = slot_of(own_s) * block + (slot_s & 1) * RANKS + number_s
    comes = jnp.where(sub[:, :1] >= half, comes, -1)
    picker = jnp.where(iota((rows, replicas * block), 1) == comes, 1.0, 0.0).astype(BF16)

    feat_in.wait()
    chosen = dot(chooser, feat[...])
    lanes = piece // HD
    for p in range(pieces):
        for b in range(lanes):
            at = p * piece + b * HD
            x32[b, pl.ds(p, sent, stride=pieces), :] = chosen[:, at : at + HD]
    for b in range(lanes):
        tx[:, :, b * HD : (b + 1) * HD] = x32[b].astype(BF16).reshape(replicas, -1, HD)

    pl.semaphore_wait(barrier, replicas)
    out_copies = [None]
    for k in range(1, replicas):
        copy = pltpu.make_async_remote_copy(
            src_ref=tx.at[k], dst_ref=rx.at[k],
            send_sem=tx_sem.at[k], recv_sem=rx_sem.at[k],
            device_id={"replica": partner(order[k], 1)}, device_id_type=MESH,
        )
        copy.start()
        out_copies.append(copy)
    rx[0] = tx[0]

    down_in.wait()
    shrunk = dot(feat[...], down[...].reshape(flat, width), NT)
    res_in.wait()
    res_s = spread(res_ref, half, (rows, flat), 0, 0)
    shrunk = jnp.where((iota((rows, flat), 1) // rank) == res_s, shrunk, 0.0)[:half]
    base = jnp.zeros((rows, 2 * cols), F32)
    for c in range(CHUNKS):
        vm_in[c].wait()
        base += dot(feat[:, c * depth : (c + 1) * depth], vm[c * depth : (c + 1) * depth, :])
    padded = jnp.concatenate([shrunk, jnp.zeros((half, cols - flat), F32)], axis=1)
    for t in range(2):
        half_tx[t, :rows] = base[:, t * cols : (t + 1) * cols]
        half_tx[t, rows:] = padded
    half_copy = pltpu.make_async_remote_copy(
        src_ref=half_tx.at[1 - core], dst_ref=half_rx,
        send_sem=peer_sem.at[0], recv_sem=peer_sem.at[1],
        device_id={"tensor": 1 - core}, device_id_type=MESH,
    )
    half_copy.start()

    q_in.wait()
    nk_in.wait()
    for h in range(heads):
        g = h // group
        q3[pl.ds(h, rows, stride=heads), :] = q[:, h * HD : (h + 1) * HD].astype(F32)
        nk3[pl.ds(h, rows, stride=heads), :] = nk[:, g * HD : (g + 1) * HD].astype(F32)
    len_in.wait()
    scale = 1.0 / math.sqrt(HD)
    head_of = iota((heads, HD), 0) // group
    place = iota((heads, ctx), 1)
    unroll = 6

    def score(base_row):
        for u in range(unroll):
            r = base_row + u
            rows_r = q3[pl.ds(pl.multiple_of(r * heads, heads), heads), :]
            wide = jnp.concatenate(
                [jnp.where(head_of == g, rows_r, 0.0) for g in range(kv)], axis=1
            ).astype(BF16)
            s = dot(wide, kc[r], NT) * scale
            sc[r] = jnp.where(place < len_ref[r], s, -jnp.inf)

    for c in range(CHUNKS):
        k_in[c].wait()
        lax.fori_loop(
            0, step // unroll, lambda i, _, c=c: score(c * step + i * unroll), None
        )

    batch = replicas // BATCHES
    batch_rows = batch * per_pair
    shr_tx[...] = jnp.zeros_like(shr_tx)

    def shrink_batch(n):
        mine = slice(n * batch, (n + 1) * batch)
        for copy in out_copies[mine]:
            if copy is not None:
                copy.wait_recv()
        first = n * batch_rows * pieces
        for b in range(lanes):
            x32[b, pl.ds(first, batch_rows * pieces), :] = (
                rx[mine, :, b * HD : (b + 1) * HD].reshape(batch_rows * pieces, HD).astype(F32)
            )
        foreign = jnp.zeros((batch_rows, flat), F32)
        for p in range(pieces):
            x_p = [x32[b, pl.ds(first + p, batch_rows, stride=pieces), :] for b in range(lanes)]
            x_p = jnp.concatenate(x_p, axis=1).astype(BF16)
            foreign += dot(x_p, down[:, :, p * piece : (p + 1) * piece].reshape(flat, piece), NT)
        shr_tx[n, :batch_rows, :flat] = foreign
        copy = pltpu.make_async_remote_copy(
            src_ref=shr_tx.at[n], dst_ref=shr_rx.at[n],
            send_sem=peer_sem.at[2 + 2 * n], recv_sem=peer_sem.at[3 + 2 * n],
            device_id={"tensor": 1 - core}, device_id_type=MESH,
        )
        copy.start()
        return copy

    shr_copies = [shrink_batch(0)]
    for n in range(1, BATCHES):
        shr_copies.append(shrink_batch(n))

    up_in.wait()
    rows_in.wait()
    count_in.wait()
    shape = (batch * block, batch_rows)
    sub_e, lane_e = iota(shape, 0), iota(shape, 1)
    place_e = sub_e & (RANKS - 1)
    expand = ((sub_e // block) * per_pair + place_e == lane_e) & (place_e < per_pair)
    expand = jnp.where(expand, 1.0, 0.0).astype(BF16)
    up_flat = up[...].reshape(flat, cols)
    ret_copies = [None]

    def return_batch(n):
        shape = (batch * block, flat)
        sub, lane = iota(shape, 0), iota(shape, 1)
        adapter = jnp.full(shape, -1, I32)
        for i in range(batch):
            source = partner(order[n * batch + i], -1)
            for s in range(PANEL_SLOTS):
                at = (sub // RANKS) == i * PANEL_SLOTS + s
                value = jnp.where(s < count_ref[0, source], rows_ref[0, s, source], -1)
                adapter = jnp.where(at, value, adapter)
        keep = (lane // rank) == adapter
        shr_copies[n].wait_recv()
        high, low = split(shr_tx[n, :batch_rows, :flat] + shr_rx[n, :batch_rows, :flat])
        high = jnp.where(keep, dot(expand, high), 0.0).astype(BF16)
        low = jnp.where(keep, dot(expand, low), 0.0).astype(BF16)
        delta = dot(high, up_flat) + dot(low, up_flat)
        ret_tx[n * batch : (n + 1) * batch] = delta.reshape(batch, block, cols)
        for k in range(max(1, n * batch), (n + 1) * batch):
            copy = pltpu.make_async_remote_copy(
                src_ref=ret_tx.at[k], dst_ref=ret_rx.at[k],
                send_sem=ret_tx_sem.at[k], recv_sem=ret_rx_sem.at[k],
                device_id={"replica": partner(order[k], -1)}, device_id_type=MESH,
            )
            copy.start()
            ret_copies.append(copy)

    for n in range(BATCHES):
        return_batch(n)
    ret_rx[0] = ret_tx[0]
    def soften(c):
        r = pl.ds(c * step, step)
        flat_r = pl.ds(c * step * heads, step * heads)
        s = sc[r].reshape(step * heads, ctx)
        fs = jnp.sum(q3[flat_r, :] * nk3[flat_r, :], axis=1, keepdims=True) * scale
        top = jnp.maximum(jnp.max(s, axis=1, keepdims=True), fs)
        w = jnp.exp(s - top)
        fw = jnp.exp(fs - top)
        inverse = 1.0 / (jnp.sum(w, axis=1, keepdims=True) + fw)
        wt[r] = (w * inverse).astype(BF16).reshape(step, heads, ctx)
        fw = (fw * inverse).astype(BF16).astype(F32)
        fresh[flat_r, :] = jnp.broadcast_to(fw, (step * heads, HD))

    for c in range(CHUNKS):
        soften(c)

    def gather(base_row):
        for u in range(unroll):
            r = base_row + u
            mixed = dot(wt[r], vc[r])
            out = mixed[:, :HD]
            for g in range(1, kv):
                out = jnp.where(head_of == g, mixed[:, g * HD : (g + 1) * HD], out)
            acc[pl.ds(pl.multiple_of(r * heads, heads), heads), :] = out

    for c in range(CHUNKS):
        v_in[c].wait()
        lax.fori_loop(
            0, step // unroll, lambda i, _, c=c: gather(c * step + i * unroll), None
        )

    half_copy.wait_recv()
    both = half_tx[core] + half_rx[...]
    high, low = split(both[rows:, :flat])
    resident = dot(high, up_flat) + dot(low, up_flat)
    resident = jnp.concatenate([resident, jnp.zeros((rows - half, cols), F32)], axis=0)
    for copy in ret_copies[1:]:
        copy.wait_recv()
    high, low = split(ret_rx[...].reshape(replicas * block, cols))
    adapted = resident + (dot(picker, high) + dot(picker, low))
    values = (both[:rows] + ADAPTER_SCALE * adapted).astype(BF16)
    nv_ref[...] = values
    values = values.astype(F32)
    for h in range(heads):
        g = h // group
        at = pl.ds(h, rows, stride=heads)
        out = acc[at, :] + fresh[at, :] * values[:, g * HD : (g + 1) * HD]
        att_ref[:, h * HD : (h + 1) * HD] = out.astype(BF16)

    for copy in out_copies[1:] + ret_copies[1:] + shr_copies + [half_copy]:
        copy.wait_send()


def body(
    features, value_matrix, adapter_down, adapter_up, queries, new_key_rows, stored_key_cache,
    stored_value_cache, cache_length, resident_adapter_index, panel_owner_slot, outgoing_rows,
    outgoing_counts,
):
    replicas = lax.axis_size("replica")
    rows, width = features.shape
    half = resident_adapter_index.shape[0]
    cols = adapter_up.shape[2]
    heads = queries.shape[1] // HD
    ctx = stored_key_cache.shape[1]
    per_pair = max(2, -(-half // replicas))
    pieces = 16 // math.gcd(16, per_pair)
    sent = replicas * per_pair
    block = PANEL_SLOTS * RANKS
    anywhere = pl.BlockSpec(memory_space=pl.ANY)
    vmem = pl.BlockSpec(memory_space=pltpu.VMEM)
    big = [features, value_matrix, adapter_down, adapter_up, queries, new_key_rows,
           stored_key_cache, stored_value_cache]
    small = [cache_length, resident_adapter_index, panel_owner_slot,
             jnp.swapaxes(outgoing_rows, 1, 2), outgoing_counts]
    dma = pltpu.SemaphoreType.DMA
    chunk = (replicas, per_pair * pieces, width // pieces)
    return pl.pallas_call(
        functools.partial(kernel, replicas, per_pair, pieces),
        out_shape=(
            jax.ShapeDtypeStruct((rows, cols), BF16),
            jax.ShapeDtypeStruct(queries.shape, BF16),
        ),
        in_specs=[anywhere] * 13,
        out_specs=(vmem, vmem),
        scratch_shapes=[pltpu.VMEM(a.shape, BF16) for a in big] + [
            pltpu.VMEM((width // pieces // HD, sent * pieces, HD), F32),
            pltpu.VMEM(chunk, BF16),
            pltpu.VMEM(chunk, BF16),
            pltpu.VMEM((2, rows + half, cols), F32),
            pltpu.VMEM((rows + half, cols), F32),
            pltpu.VMEM((BATCHES, -(-sent // BATCHES // 8) * 8, HD), F32),
            pltpu.VMEM((BATCHES, -(-sent // BATCHES // 8) * 8, HD), F32),
            pltpu.VMEM((replicas, block, cols), F32),
            pltpu.VMEM((replicas, block, cols), F32),
            pltpu.VMEM((rows * heads, HD), F32),
            pltpu.VMEM((rows * heads, HD), F32),
            pltpu.VMEM((rows, heads, ctx), F32),
            pltpu.VMEM((rows, heads, ctx), BF16),
            pltpu.VMEM((rows * heads, HD), F32),
            pltpu.VMEM((rows * heads, HD), F32),
            *[pltpu.SMEM(a.shape, I32) for a in small],
            dma((10,)), dma((CHUNKS,)), dma((CHUNKS,)), dma((CHUNKS,)),
            dma((replicas,)), dma((replicas,)), dma((replicas,)), dma((replicas,)), dma((2 + 2 * BATCHES,)),
        ],
        compiler_params=pltpu.CompilerParams(
            collective_id=0, has_side_effects=True, vmem_limit_bytes=40 * 1024 * 1024
        ),
        cost_estimate=pl.CostEstimate(
            flops=500_000_000, bytes_accessed=12_000_000, transcendentals=100_000
        ),
    )(*[pltpu.with_memory_space_constraint(a, pltpu.HBM) for a in big + small])


def solution(mesh):
    in_specs = (
        P(("groups", "replica"), "tensor"),
        P("tensor", None),
        P("replica", None, "tensor"),
        P("replica", None, "tensor"),
        P(("groups", "replica"), "tensor"),
        P(("groups", "replica"), "tensor"),
        P(("groups", "replica"), None, "tensor"),
        P(("groups", "replica"), None, "tensor"),
        P(("groups", "replica")),
        P(("groups", "replica")),
        P(("groups", "replica")),
        P(("groups", "replica"), None, None),
        P(("groups", "replica"), None),
    )
    out_specs = (P(("groups", "replica"), "tensor"), P(("groups", "replica"), "tensor"))
    return jax.shard_map(body, mesh=mesh, in_specs=in_specs, out_specs=out_specs, check_vma=False)
```

```python
import functools
import math

import jax
import jax.numpy as jnp
from jax import lax
from jax.experimental import pallas as pl
from jax.experimental.pallas import tpu as pltpu
from jax.sharding import PartitionSpec as P

HD = 128
PANEL_SLOTS = 2
ADAPTER_SCALE = 2.0
MESH = pl.DeviceIdType.MESH
F32, BF16, I32 = jnp.float32, jnp.bfloat16, jnp.int32
NT = (((1,), (1,)), ((), ()))
RANKS = 4
CHUNKS = 2
BATCHES = 2


def iota(shape, axis):
    return lax.broadcasted_iota(I32, shape, axis)


def dot(a, b, dims=(((1,), (0,)), ((), ()))):
    return lax.dot_general(a, b, dims, preferred_element_type=F32)


def split(x):
    high = x.astype(BF16)
    return high, (x - high.astype(F32)).astype(BF16)


def spread(ref, count, shape, axis, first):
    index = iota(shape, axis)
    out = jnp.full(shape, -1, I32)
    for i in range(count):
        out = jnp.where(index == first + i, ref[i], out)
    return out


def kernel(
    replicas, per_pair, pieces,
    feat_hbm, vm_hbm, down_hbm, up_hbm, q_hbm, nk_hbm, k_hbm, v_hbm,
    len_hbm, res_hbm, slot_hbm, rows_hbm, count_hbm,
    nv_ref, att_ref,
    feat, vm, down, up, q, nk, kc, vc,
    x32, tx, rx, half_tx, half_rx, shr_tx, shr_rx, ret_tx, ret_rx,
    q3, nk3, sc, wt, fresh, acc,
    len_ref, res_ref, slot_ref, rows_ref, count_ref,
    in_sem, vm_sem, k_sem, v_sem, tx_sem, rx_sem, ret_tx_sem, ret_rx_sem, peer_sem,
):
    me = lax.axis_index("replica")
    core = lax.axis_index("tensor")
    rows, width = feat.shape
    half = res_ref.shape[0]
    adapters, rank, _ = down.shape
    flat = adapters * rank
    cols = up.shape[2]
    kv = nk.shape[1] // HD
    heads = q.shape[1] // HD
    group = heads // kv
    ctx = kc.shape[1]
    piece = width // pieces
    sent = replicas * per_pair
    block = PANEL_SLOTS * RANKS
    step = rows // CHUNKS
    depth = width // CHUNKS

    barrier = pltpu.get_barrier_semaphore()
    for d in range(1, replicas):
        pl.semaphore_signal(
            barrier, inc=1, device_id={"replica": lax.rem(me + d, replicas)}, device_id_type=MESH
        )
    pl.semaphore_signal(barrier, inc=1, device_id={"tensor": 1 - core}, device_id_type=MESH)

    def load(src, dst, sem):
        copy = pltpu.make_async_copy(src, dst, sem)
        copy.start()
        return copy

    slot_in = load(slot_hbm, slot_ref, in_sem.at[5])
    feat_in = load(feat_hbm, feat, in_sem.at[0])
    down_in = load(down_hbm, down, in_sem.at[1])
    vm_in = [
        load(vm_hbm.at[pl.ds(c * depth, depth)], vm.at[pl.ds(c * depth, depth)], vm_sem.at[c])
        for c in range(CHUNKS)
    ]
    q_in = load(q_hbm, q, in_sem.at[2])
    nk_in = load(nk_hbm, nk, in_sem.at[3])
    k_in = [
        load(k_hbm.at[pl.ds(c * step, step)], kc.at[pl.ds(c * step, step)], k_sem.at[c])
        for c in range(CHUNKS)
    ]
    up_in = load(up_hbm, up, in_sem.at[4])
    res_in = load(res_hbm, res_ref, in_sem.at[6])
    len_in = load(len_hbm, len_ref, in_sem.at[7])
    rows_in = load(rows_hbm, rows_ref, in_sem.at[8])
    count_in = load(count_hbm, count_ref, in_sem.at[9])
    v_in = [
        load(v_hbm.at[pl.ds(c * step, step)], vc.at[pl.ds(c * step, step)], v_sem.at[c])
        for c in range(CHUNKS)
    ]

    order = [0] + sorted(range(1, replicas), key=lambda k: -abs(2 * k - replicas))

    def partner(offset, sign):
        return lax.rem(me + sign * offset + replicas, replicas)

    def slot_of(owner):
        offset = jnp.where(owner < me, owner - me + replicas, owner - me)
        out = jnp.zeros_like(owner)
        for k in range(1, replicas):
            out = jnp.where(offset == order[k], k, out)
        return out

    square = (rows, rows)
    sub, lane = iota(square, 0), iota(square, 1)
    slot_in.wait()
    slot_l = spread(slot_ref, half, (1, rows), 1, half)
    slot_s = jnp.sum(jnp.where(sub == lane, slot_l, 0).astype(F32), axis=1, keepdims=True)
    slot_s = slot_s.astype(I32)
    own_l, own_s = slot_l >> 1, slot_s >> 1
    same = own_l == own_s
    number_l = jnp.sum(jnp.where(same & (sub < lane), 1.0, 0.0), axis=0, keepdims=True).astype(I32)
    number_s = jnp.sum(jnp.where(same & (lane < sub), 1.0, 0.0), axis=1, keepdims=True).astype(I32)
    goes = jnp.where(lane[:1] >= half, slot_of(own_l) * per_pair + number_l, -1)
    chooser = jnp.where(iota((sent, rows), 0) == goes, 1.0, 0.0).astype(BF16)
    comes = slot_of(own_s) * block + (slot_s & 1) * RANKS + number_s
    comes = jnp.where(sub[:, :1] >= half, comes, -1)
    picker = jnp.where(iota((rows, replicas * block), 1) == comes, 1.0, 0.0).astype(BF16)

    feat_in.wait()
    chosen = dot(chooser, feat[...])
    lanes = piece // HD
    for p in range(pieces):
        for b in range(lanes):
            at = p * piece + b * HD
            x32[b, pl.ds(p, sent, stride=pieces), :] = chosen[:, at : at + HD]
    for b in range(lanes):
        tx[:, :, b * HD : (b + 1) * HD] = x32[b].astype(BF16).reshape(replicas, -1, HD)

    pl.semaphore_wait(barrier, replicas)
    out_copies = [None]
    for k in range(1, replicas):
        copy = pltpu.make_async_remote_copy(
            src_ref=tx.at[k], dst_ref=rx.at[k],
            send_sem=tx_sem.at[k], recv_sem=rx_sem.at[k],
            device_id={"replica": partner(order[k], 1)}, device_id_type=MESH,
        )
        copy.start()
        out_copies.append(copy)
    rx[0] = tx[0]

    down_in.wait()
    shrunk = dot(feat[...], down[...].reshape(flat, width), NT)
    res_in.wait()
    res_s = spread(res_ref, half, (rows, flat), 0, 0)
    shrunk = jnp.where((iota((rows, flat), 1) // rank) == res_s, shrunk, 0.0)[:half]
    base = jnp.zeros((rows, 2 * cols), F32)
    for c in range(CHUNKS):
        vm_in[c].wait()
        base += dot(feat[:, c * depth : (c + 1) * depth], vm[c * depth : (c + 1) * depth, :])
    padded = jnp.concatenate([shrunk, jnp.zeros((half, cols - flat), F32)], axis=1)
    for t in range(2):
        half_tx[t, :rows] = base[:, t * cols : (t + 1) * cols]
        half_tx[t, rows:] = padded
    half_copy = pltpu.make_async_remote_copy(
        src_ref=half_tx.at[1 - core], dst_ref=half_rx,
        send_sem=peer_sem.at[0], recv_sem=peer_sem.at[1],
        device_id={"tensor": 1 - core}, device_id_type=MESH,
    )
    half_copy.start()

    q_in.wait()
    nk_in.wait()
    for h in range(heads):
        g = h // group
        q3[pl.ds(h, rows, stride=heads), :] = q[:, h * HD : (h + 1) * HD].astype(F32)
        nk3[pl.ds(h, rows, stride=heads), :] = nk[:, g * HD : (g + 1) * HD].astype(F32)
    len_in.wait()
    scale = 1.0 / math.sqrt(HD)
    head_of = iota((heads, HD), 0) // group
    place = iota((heads, ctx), 1)
    unroll = 6

    def score(base_row):
        for u in range(unroll):
            r = base_row + u
            rows_r = q3[pl.ds(pl.multiple_of(r * heads, heads), heads), :]
            wide = jnp.concatenate(
                [jnp.where(head_of == g, rows_r, 0.0) for g in range(kv)], axis=1
            ).astype(BF16)
            s = dot(wide, kc[r], NT) * scale
            sc[r] = jnp.where(place < len_ref[r], s, -jnp.inf)

    for c in range(CHUNKS):
        k_in[c].wait()
        lax.fori_loop(
            0, step // unroll, lambda i, _, c=c: score(c * step + i * unroll), None
        )

    batch = replicas // BATCHES
    batch_rows = batch * per_pair
    shr_tx[...] = jnp.zeros_like(shr_tx)

    def shrink_batch(n):
        mine = slice(n * batch, (n + 1) * batch)
        for copy in out_copies[mine]:
            if copy is not None:
                copy.wait_recv()
        first = n * batch_rows * pieces
        for b in range(lanes):
            x32[b, pl.ds(first, batch_rows * pieces), :] = (
                rx[mine, :, b * HD : (b + 1) * HD].reshape(batch_rows * pieces, HD).astype(F32)
            )
        foreign = jnp.zeros((batch_rows, flat), F32)
        for p in range(pieces):
            x_p = [x32[b, pl.ds(first + p, batch_rows, stride=pieces), :] for b in range(lanes)]
            x_p = jnp.concatenate(x_p, axis=1).astype(BF16)
            foreign += dot(x_p, down[:, :, p * piece : (p + 1) * piece].reshape(flat, piece), NT)
        shr_tx[n, :batch_rows, :flat] = foreign
        copy = pltpu.make_async_remote_copy(
            src_ref=shr_tx.at[n], dst_ref=shr_rx.at[n],
            send_sem=peer_sem.at[2 + 2 * n], recv_sem=peer_sem.at[3 + 2 * n],
            device_id={"tensor": 1 - core}, device_id_type=MESH,
        )
        copy.start()
        return copy

    shr_copies = [shrink_batch(0)]
    for n in range(1, BATCHES):
        shr_copies.append(shrink_batch(n))

    up_in.wait()
    rows_in.wait()
    count_in.wait()
    shape = (batch * block, batch_rows)
    sub_e, lane_e = iota(shape, 0), iota(shape, 1)
    place_e = sub_e & (RANKS - 1)
    expand = ((sub_e // block) * per_pair + place_e == lane_e) & (place_e < per_pair)
    expand = jnp.where(expand, 1.0, 0.0).astype(BF16)
    up_flat = up[...].reshape(flat, cols)
    ret_copies = [None]

    def return_batch(n):
        shape = (batch * block, flat)
        sub, lane = iota(shape, 0), iota(shape, 1)
        adapter = jnp.full(shape, -1, I32)
        for i in range(batch):
            source = partner(order[n * batch + i], -1)
            for s in range(PANEL_SLOTS):
                at = (sub // RANKS) == i * PANEL_SLOTS + s
                value = jnp.where(s < count_ref[0, source], rows_ref[0, s, source], -1)
                adapter = jnp.where(at, value, adapter)
        keep = (lane // rank) == adapter
        shr_copies[n].wait_recv()
        high, low = split(shr_tx[n, :batch_rows, :flat] + shr_rx[n, :batch_rows, :flat])
        high = jnp.where(keep, dot(expand, high), 0.0).astype(BF16)
        low = jnp.where(keep, dot(expand, low), 0.0).astype(BF16)
        delta = dot(high, up_flat) + dot(low, up_flat)
        ret_tx[n * batch : (n + 1) * batch] = delta.reshape(batch, block, cols)
        for k in range(max(1, n * batch), (n + 1) * batch):
            copy = pltpu.make_async_remote_copy(
                src_ref=ret_tx.at[k], dst_ref=ret_rx.at[k],
                send_sem=ret_tx_sem.at[k], recv_sem=ret_rx_sem.at[k],
                device_id={"replica": partner(order[k], -1)}, device_id_type=MESH,
            )
            copy.start()
            ret_copies.append(copy)

    for n in range(BATCHES):
        return_batch(n)
    ret_rx[0] = ret_tx[0]
    def soften(c):
        r = pl.ds(c * step, step)
        flat_r = pl.ds(c * step * heads, step * heads)
        s = sc[r].reshape(step * heads, ctx)
        fs = jnp.sum(q3[flat_r, :] * nk3[flat_r, :], axis=1, keepdims=True) * scale
        top = jnp.maximum(jnp.max(s, axis=1, keepdims=True), fs)
        w = jnp.exp(s - top)
        fw = jnp.exp(fs - top)
        inverse = 1.0 / (jnp.sum(w, axis=1, keepdims=True) + fw)
        wt[r] = (w * inverse).astype(BF16).reshape(step, heads, ctx)
        fw = (fw * inverse).astype(BF16).astype(F32)
        fresh[flat_r, :] = jnp.broadcast_to(fw, (step * heads, HD))

    for c in range(CHUNKS):
        soften(c)

    def gather(base_row):
        for u in range(unroll):
            r = base_row + u
            mixed = dot(wt[r], vc[r])
            out = mixed[:, :HD]
            for g in range(1, kv):
                out = jnp.where(head_of == g, mixed[:, g * HD : (g + 1) * HD], out)
            acc[pl.ds(pl.multiple_of(r * heads, heads), heads), :] = out

    for c in range(CHUNKS):
        v_in[c].wait()
        lax.fori_loop(
            0, step // unroll, lambda i, _, c=c: gather(c * step + i * unroll), None
        )

    half_copy.wait_recv()
    both = half_tx[core] + half_rx[...]
    high, low = split(both[rows:, :flat])
    resident = dot(high, up_flat) + dot(low, up_flat)
    resident = jnp.concatenate([resident, jnp.zeros((rows - half, cols), F32)], axis=0)
    for copy in ret_copies[1:]:
        copy.wait_recv()
    high, low = split(ret_rx[...].reshape(replicas * block, cols))
    adapted = resident + (dot(picker, high) + dot(picker, low))
    values = (both[:rows] + ADAPTER_SCALE * adapted).astype(BF16)
    nv_ref[...] = values
    values = values.astype(F32)
    for h in range(heads):
        g = h // group
        at = pl.ds(h, rows, stride=heads)
        out = acc[at, :] + fresh[at, :] * values[:, g * HD : (g + 1) * HD]
        att_ref[:, h * HD : (h + 1) * HD] = out.astype(BF16)

    for copy in out_copies[1:] + ret_copies[1:] + shr_copies + [half_copy]:
        copy.wait_send()


def body(
    features, value_matrix, adapter_down, adapter_up, queries, new_key_rows, stored_key_cache,
    stored_value_cache, cache_length, resident_adapter_index, panel_owner_slot, outgoing_rows,
    outgoing_counts,
):
    replicas = lax.axis_size("replica")
    rows, width = features.shape
    half = resident_adapter_index.shape[0]
    cols = adapter_up.shape[2]
    heads = queries.shape[1] // HD
    ctx = stored_key_cache.shape[1]
    per_pair = max(2, -(-half // replicas))
    pieces = 16 // math.gcd(16, per_pair)
    sent = replicas * per_pair
    block = PANEL_SLOTS * RANKS
    anywhere = pl.BlockSpec(memory_space=pl.ANY)
    vmem = pl.BlockSpec(memory_space=pltpu.VMEM)
    big = [features, value_matrix, adapter_down, adapter_up, queries, new_key_rows,
           stored_key_cache, stored_value_cache]
    small = [cache_length, resident_adapter_index, panel_owner_slot,
             jnp.swapaxes(outgoing_rows, 1, 2), outgoing_counts]
    dma = pltpu.SemaphoreType.DMA
    chunk = (replicas, per_pair * pieces, width // pieces)
    return pl.pallas_call(
        functools.partial(kernel, replicas, per_pair, pieces),
        out_shape=(
            jax.ShapeDtypeStruct((rows, cols), BF16),
            jax.ShapeDtypeStruct(queries.shape, BF16),
        ),
        in_specs=[anywhere] * 13,
        out_specs=(vmem, vmem),
        scratch_shapes=[pltpu.VMEM(a.shape, BF16) for a in big] + [
            pltpu.VMEM((width // pieces // HD, sent * pieces, HD), F32),
            pltpu.VMEM(chunk, BF16),
            pltpu.VMEM(chunk, BF16),
            pltpu.VMEM((2, rows + half, cols), F32),
            pltpu.VMEM((rows + half, cols), F32),
            pltpu.VMEM((BATCHES, -(-sent // BATCHES // 8) * 8, HD), F32),
            pltpu.VMEM((BATCHES, -(-sent // BATCHES // 8) * 8, HD), F32),
            pltpu.VMEM((replicas, block, cols), F32),
            pltpu.VMEM((replicas, block, cols), F32),
            pltpu.VMEM((rows * heads, HD), F32),
            pltpu.VMEM((rows * heads, HD), F32),
            pltpu.VMEM((rows, heads, ctx), F32),
            pltpu.VMEM((rows, heads, ctx), BF16),
            pltpu.VMEM((rows * heads, HD), F32),
            pltpu.VMEM((rows * heads, HD), F32),
            *[pltpu.SMEM(a.shape, I32) for a in small],
            dma((10,)), dma((CHUNKS,)), dma((CHUNKS,)), dma((CHUNKS,)),
            dma((replicas,)), dma((replicas,)), dma((replicas,)), dma((replicas,)), dma((2 + 2 * BATCHES,)),
        ],
        compiler_params=pltpu.CompilerParams(
            collective_id=0, has_side_effects=True, vmem_limit_bytes=40 * 1024 * 1024
        ),
        cost_estimate=pl.CostEstimate(
            flops=500_000_000, bytes_accessed=12_000_000, transcendentals=100_000
        ),
    )(*[pltpu.with_memory_space_constraint(a, pltpu.HBM) for a in big + small])


def solution(mesh):
    in_specs = (
        P(("groups", "replica"), "tensor"),
        P("tensor", None),
        P("replica", None, "tensor"),
        P("replica", None, "tensor"),
        P(("groups", "replica"), "tensor"),
        P(("groups", "replica"), "tensor"),
        P(("groups", "replica"), None, "tensor"),
        P(("groups", "replica"), None, "tensor"),
        P(("groups", "replica")),
        P(("groups", "replica")),
        P(("groups", "replica")),
        P(("groups", "replica"), None, None),
        P(("groups", "replica"), None),
    )
    out_specs = (P(("groups", "replica"), "tensor"), P(("groups", "replica"), "tensor"))
    return jax.shard_map(body, mesh=mesh, in_specs=in_specs, out_specs=out_specs, check_vma=False)
```
